128 devices in a mesh: items: 2 (over z_lo), tower: 64 (over x, z_hi, y, core).
Axes of the slice: x: 4, y: 4, z: 4 (z_hi: 2, z_lo: 2; z = z_hi * 2 + z_lo), core: 2. Of those that a mesh axis runs over, the one named last changes fastest.
Arguments:
- side_states: bfloat16 [2, 64, 2, 336, 768], P('items', 'tower'), may hold values from -6 to 6
- assignment: int32 [2, 32], P('items'), may hold values from 0 to 1
- image_class: int32 [2, 32, 2], P('items'), may hold values from 0 to 1
- caption_length: int32 [2, 32, 2], P('items'), may hold values from 4 to 336, as said below
- cls_token: bfloat16 [768], replicated, may hold values from -6 to 6
- proj_weight: bfloat16 [2, 768, 768], replicated, may hold values from -0.21875 to 0.21875
- proj_bias: bfloat16 [2, 768], replicated, may hold values from -4 to 4
- attn_gain: bfloat16 [768], replicated, may hold values from 0.25 to 1.75
- attn_shift: bfloat16 [768], replicated, may hold values from -4 to 4
- qkv_weight: bfloat16 [768, 2304], replicated, may hold values from -0.3125 to 0.3125
- query_bias: bfloat16 [768], replicated, may hold values from -6 to 6
- value_bias: bfloat16 [768], replicated, may hold values from -6 to 6
- out_weight: bfloat16 [768, 768], replicated, may hold values from -0.4375 to 0.4375
- out_bias: bfloat16 [768], replicated, may hold values from -4 to 4
- mlp_gain: bfloat16 [768], replicated, may hold values from 0.25 to 1.75
- mlp_shift: bfloat16 [768], replicated, may hold values from -4 to 4
- up_weight: bfloat16 [768, 3072], replicated, may hold values from -0.21875 to 0.21875
- up_bias: bfloat16 [3072], replicated, may hold values from -4 to 4
- down_weight: bfloat16 [3072, 768], replicated, may hold values from -0.15625 to 0.15625
- down_bias: bfloat16 [768], replicated, may hold values from -4 to 4
- out_cotangent: bfloat16 [2, 64, 673, 768], P('items', 'tower'), may hold values from -6 to 6
Outputs:
- layer_out: bfloat16 [2, 64, 673, 768], P('items', 'tower')
- states_grad: bfloat16 [2, 64, 2, 336, 768], P('items', 'tower')
- cls_grad: float32 [768], replicated
- proj_weight_grad: float32 [2, 768, 768], replicated
- proj_bias_grad: float32 [2, 768], replicated
- attn_gain_grad: float32 [768], replicated
- attn_shift_grad: float32 [768], replicated
- qkv_weight_grad: float32 [768, 2304], replicated
- query_bias_grad: float32 [768], replicated
- value_bias_grad: float32 [768], replicated
- out_weight_grad: float32 [768, 768], replicated
- out_bias_grad: float32 [768], replicated
- mlp_gain_grad: float32 [768], replicated
- mlp_shift_grad: float32 [768], replicated
- up_weight_grad: float32 [768, 3072], replicated
- up_bias_grad: float32 [3072], replicated
- down_weight_grad: float32 [3072, 768], replicated
- down_bias_grad: float32 [768], replicated
The draws below stay inside these ranges and needn't reach their ends.
Inputs may be any that keep to these rules, and one draw needn't show every extreme that they name: assignment picks which item of a pair the image-side device assembles; the other goes to the caption-side device. `image_class`: 0 for an image of 197 tokens, 1 for one of 325. `caption_length`: some caption in every draw has 336 tokens.
All inputs are finite; a program needn't handle non-finite values.
Results may differ from the reference program's by a relative error of at most 0.017.
The reference program's roundings to bfloat16 on the way count: a program that leaves them out, or rounds other values in their place, can miss the bound.
Values may be sent and summed in bfloat16 or wider, within the bound.
A program may use at most 320 MiB of HBM per device.

```python
import jax
import jax.numpy as jnp
from jax import lax

D = 768
HEADS = 12
FF = 3072
HEAD_DIM = 64
SMALL_PATCHES = 197
LARGE_PATCHES = 325
SLOT = 336
SEQ = 673
N_ITEMS = 2
N_TOWER = 64


def draw_caption_length(key, part):
    key = jax.random.fold_in(key, 7)
    first_key, second_key = jax.random.split(key)
    count = N_ITEMS * (N_TOWER // 2) * 2
    lengths = jax.random.randint(first_key, (count,), 4, SLOT + 1)
    longest = jax.random.randint(second_key, (), 0, count)
    lengths = jnp.where(jnp.arange(count) == longest, SLOT, lengths)
    return lengths.reshape(N_ITEMS, N_TOWER // 2, 2).astype(jnp.int32)


def touch_ends(result, key, low, largest):
    place = [jax.random.randint(jax.random.fold_in(key, axis), (), 0, length) for axis, length in enumerate(result.shape)]
    widest = result.shape.index(max(result.shape))
    beside = place[:widest] + [(place[widest] + 1) % result.shape[widest]] + place[widest + 1:]
    return result.at[tuple(place)].set(low).at[tuple(beside)].set(largest)


def levels(own_key, shape, shards, smallest, largest):
    level, own = 1.0, jax.random.fold_in(own_key, 6)
    for dim, shards_of in shards:
        steps = jnp.exp(jax.random.uniform(jax.random.fold_in(own, dim), (shards_of,), jnp.float32, smallest / len(shards), largest / len(shards)))
        level = level * jnp.repeat(steps, shape[dim] // shards_of).reshape([-1 if axis == dim else 1 for axis in range(len(shape))])
    return level


def scatter_about(own_key, extent, scale, reach, cuts=(), kind=jnp.bfloat16):
    factor_of = levels(own_key, extent, cuts, -0.22, 0.18) if cuts else 1.0
    entries = jax.random.normal(own_key, extent, jnp.float32) * scale * factor_of
    return jnp.minimum(jnp.maximum(entries, -reach), reach).astype(kind)


def setup_inputs(seed: int = 0) -> dict:
    arg_keys = jax.random.split(jax.random.key(seed), 22)
    return {
        "side_states": scatter_about(arg_keys[0], (N_ITEMS, N_TOWER, 2, SLOT, D), 1.0, 6.0, ((0, 2), (1, 64))),
        "assignment": touch_ends(jax.random.randint(arg_keys[1], (N_ITEMS, N_TOWER // 2), 0, 2), jax.random.fold_in(arg_keys[1], 1), 0, 1).astype(jnp.int32),
        "image_class": touch_ends(jax.random.randint(arg_keys[2], (N_ITEMS, N_TOWER // 2, 2), 0, 2), jax.random.fold_in(arg_keys[2], 1), 0, 1).astype(jnp.int32),
        "caption_length": draw_caption_length(jax.random.fold_in(arg_keys[21], 71), 0),
        "cls_token": scatter_about(arg_keys[4], (D,), 1.0, 6.0),
        "proj_weight": scatter_about(arg_keys[5], (2, D, D), D ** -0.5, 0.21875),
        "proj_bias": scatter_about(arg_keys[6], (2, D), 0.3, 4.0),
        "attn_gain": jnp.clip(1.0 + 0.15 * jax.random.normal(arg_keys[7], (D,), jnp.float32), 0.25, 1.75).astype(jnp.bfloat16),
        "attn_shift": scatter_about(arg_keys[8], (D,), 0.3, 4.0),
        "qkv_weight": scatter_about(arg_keys[9], (D, 3 * D), (D // 2) ** -0.5, 0.3125),
        "query_bias": scatter_about(arg_keys[10], (D,), 0.5, 6.0),
        "value_bias": scatter_about(arg_keys[11], (D,), 0.5, 6.0),
        "out_weight": scatter_about(arg_keys[12], (D, D), (D // 4) ** -0.5, 0.4375),
        "out_bias": scatter_about(arg_keys[13], (D,), 0.3, 4.0),
        "mlp_gain": jnp.clip(1.0 + 0.15 * jax.random.normal(arg_keys[14], (D,), jnp.float32), 0.25, 1.75).astype(jnp.bfloat16),
        "mlp_shift": scatter_about(arg_keys[15], (D,), 0.3, 4.0),
        "up_weight": scatter_about(arg_keys[16], (D, FF), D ** -0.5, 0.21875),
        "up_bias": scatter_about(arg_keys[17], (FF,), 0.3, 4.0),
        "down_weight": scatter_about(arg_keys[18], (FF, D), (FF // 2) ** -0.5, 0.15625),
        "down_bias": scatter_about(arg_keys[19], (D,), 0.3, 4.0),
        "out_cotangent": scatter_about(arg_keys[20], (N_ITEMS, N_TOWER, SEQ, D), 1.0, 6.0, ((0, 2), (1, 64))),
    }


EPSILON = 1e-05
MASKED = -1e+30

@jax.custom_vjp
def low(v):
    return lax.optimization_barrier(v.astype(jnp.bfloat16)).astype(jnp.float32)

@jax.custom_vjp
def low_back(v):
    return v

def low_keep(v):
    return (low(v), None)

def low_pass(kept, grad):
    return (grad,)

def back_keep(v):
    return (v, None)

def back_low(kept, grad):
    return (low(grad),)
low.defvjp(low_keep, low_pass)
low_back.defvjp(back_keep, back_low)

def both_round(value):
    return low_back(low(value))

def matmul(left, right):
    return jnp.dot(left, right, precision=lax.Precision.HIGHEST)

def norm_rows(hidden, gain, shift):
    center = hidden - lax.optimization_barrier(jnp.mean(hidden, axis=-1, keepdims=True))
    spread = lax.optimization_barrier(jnp.mean(center * center, axis=-1, keepdims=True))
    return center * lax.rsqrt(spread + EPSILON) * gain + shift

def encoder_layer(params, merged, valid_rows):
    cls_token, proj_weight, proj_bias, attn_gain, attn_shift, qkv_weight, query_bias, value_bias, out_weight, out_bias, mlp_gain, mlp_shift, up_weight, up_bias, down_weight, down_bias = params
    sequence = merged.shape[0]
    normed = low(norm_rows(merged, attn_gain, attn_shift))
    mixed_qkv = matmul(normed, qkv_weight)
    queries = both_round((mixed_qkv[:, :D] + query_bias) * 0.125).reshape(sequence, HEADS, HEAD_DIM)
    key_rows = both_round(mixed_qkv[:, D:2 * D]).reshape(sequence, HEADS, HEAD_DIM)
    values = both_round(mixed_qkv[:, 2 * D:] + value_bias).reshape(sequence, HEADS, HEAD_DIM)
    scores = low_back(jnp.einsum('qhd,khd->hqk', queries, key_rows, precision=lax.Precision.HIGHEST))
    scores = jnp.where(valid_rows[None, None, :] > 0.5, scores, MASKED)
    row_peak = lax.optimization_barrier(jnp.max(scores, axis=-1, keepdims=True))
    exponent = jnp.exp(scores - row_peak)
    attention_weights = low(exponent / lax.optimization_barrier(jnp.sum(exponent, axis=-1, keepdims=True)))
    attended = jnp.einsum('hqk,khd->qhd', attention_weights, values, precision=lax.Precision.HIGHEST)
    attended = both_round(attended.reshape(sequence, D))
    hidden = merged + low_back(matmul(attended, out_weight) + out_bias)
    inner_normed = low(norm_rows(hidden, mlp_gain, mlp_shift))
    gate_pre = low_back(matmul(inner_normed, up_weight) + up_bias)
    activated = low(jax.nn.gelu(gate_pre))
    branch = low_back(matmul(activated, down_weight) + down_bias)
    return (hidden + branch) * valid_rows[:, None]

def pick_item(array, index):
    return lax.dynamic_index_in_dim(array, index, 0, keepdims=False)

def group_out(params, image_pair, text_pair, chosen, classes, lengths):
    cls_token, proj_weight, proj_bias = (params[0], params[1], params[2])
    slot_rows = jnp.arange(SLOT)
    image_count = jnp.where(classes == 1, LARGE_PATCHES, SMALL_PATCHES)
    image_mask = (slot_rows[None, :] < image_count[:, None]).astype(jnp.float32)
    text_mask = (slot_rows[None, :] < lengths[:, None]).astype(jnp.float32)
    image_rows = jnp.einsum('isd,de->ise', image_pair, proj_weight[0], precision=lax.Precision.HIGHEST)
    image_rows = both_round(image_rows + proj_bias[0]) * image_mask[:, :, None]
    text_rows = jnp.einsum('isd,de->ise', text_pair, proj_weight[1], precision=lax.Precision.HIGHEST)
    text_rows = both_round(text_rows + proj_bias[1]) * text_mask[:, :, None]
    results = []
    for assembled in (chosen, 1 - chosen):
        assembled = assembled.astype(jnp.int32)
        valid_rows = jnp.concatenate([jnp.ones((1,), jnp.float32), pick_item(image_mask, assembled), pick_item(text_mask, assembled)])
        merged = jnp.concatenate([cls_token[None, :], pick_item(image_rows, assembled), pick_item(text_rows, assembled)], axis=0)
        results.append(encoder_layer(params, merged, valid_rows))
    return jnp.stack(results)

def reference(side_states, assignment, image_class, caption_length, cls_token, proj_weight, proj_bias, attn_gain, attn_shift, qkv_weight, query_bias, value_bias, out_weight, out_bias, mlp_gain, mlp_shift, up_weight, up_bias, down_weight, down_bias, out_cotangent):
    half_size = N_TOWER // 2
    groups = N_ITEMS * half_size
    params = tuple((p.astype(jnp.float32) for p in (cls_token, proj_weight, proj_bias, attn_gain, attn_shift, qkv_weight, query_bias, value_bias, out_weight, out_bias, mlp_gain, mlp_shift, up_weight, up_bias, down_weight, down_bias)))
    image_side = side_states[:, :half_size].reshape(groups, 2, SLOT, D).astype(jnp.float32)
    text_side = side_states[:, half_size:].reshape(groups, 2, SLOT, D).astype(jnp.float32)
    chosen_all = assignment.reshape(groups).astype(jnp.int32)
    classes_all = image_class.reshape(groups, 2).astype(jnp.int32)
    lengths_all = caption_length.reshape(groups, 2).astype(jnp.int32)

    def forward(weights, image_input, text_input):
        group_step = jax.checkpoint(group_out)

        def one_group(inputs):
            return group_step(weights, inputs[0], inputs[1], inputs[2], inputs[3], inputs[4])
        paired = lax.map(one_group, (image_input, text_input, chosen_all, classes_all, lengths_all))
        image_devices = paired[:, 0].reshape(N_ITEMS, half_size, SEQ, D)
        text_devices = paired[:, 1].reshape(N_ITEMS, half_size, SEQ, D)
        return jnp.concatenate([image_devices, text_devices], axis=1)
    layer_out, pullback = jax.vjp(forward, params, image_side, text_side)
    weight_grads, image_grad, text_grad = pullback(out_cotangent.astype(jnp.float32))
    states_grad = jnp.concatenate([image_grad.reshape(N_ITEMS, half_size, 2, SLOT, D), text_grad.reshape(N_ITEMS, half_size, 2, SLOT, D)], axis=1)
    cls_grad, proj_weight_grad, proj_bias_grad, attn_gain_grad, attn_shift_grad, qkv_weight_grad, query_bias_grad, value_bias_grad, out_weight_grad, out_bias_grad, mlp_gain_grad, mlp_shift_grad, up_weight_grad, up_bias_grad, down_weight_grad, down_bias_grad = weight_grads
    return (layer_out.astype(jnp.bfloat16), states_grad.astype(jnp.bfloat16), cls_grad, proj_weight_grad, proj_bias_grad, attn_gain_grad, attn_shift_grad, qkv_weight_grad, query_bias_grad, value_bias_grad, out_weight_grad, out_bias_grad, mlp_gain_grad, mlp_shift_grad, up_weight_grad, up_bias_grad, down_weight_grad, down_bias_grad)
```

```python
import jax
import jax.numpy as jnp
from jax import lax
from jax.experimental import pallas as pl
from jax.experimental.pallas import tpu as pltpu
from jax.sharding import PartitionSpec as P

bf16 = jnp.bfloat16
f32 = jnp.float32
MESH = pl.DeviceIdType.MESH
D = 768
FF = 3072
SLOT = 336
SEQ = 673
SMALL_PATCHES = 197
LARGE_PATCHES = 325
NR = 704
CLS = 2 * SLOT
EPS = 1e-5
MASKED = -1e30
MIB = 2**20

NN = (((1,), (0,)), ((), ()))
NT = (((1,), (1,)), ((), ()))
TN = (((0,), (0,)), ((), ()))


def dot(a, b, dims=NN):
    return lax.dot_general(a, b, dims, preferred_element_type=f32)


def loop(n, body, start=0):
    def step(i, carry):
        body(i)
        return carry

    lax.fori_loop(start, n, step, 0)


def span(i, n, base=0):
    return pl.ds(pl.multiple_of(base + i * n, n), n)


def row_of(ref):
    return ref[...].astype(f32).reshape(1, ref.shape[0])


def coords():
    items, tower = lax.axis_index("items"), lax.axis_index("tower")
    x, y = tower // 16, lax.rem(tower // 2, 4)
    return (x, y, lax.rem(tower // 8, 2) * 2 + items), lax.rem(tower, 2)


def device(xyz, core):
    x, y, z = xyz
    return lax.rem(z, 2), ((x * 2 + z // 2) * 4 + y) * 2 + core


def along(xyz, axis, by):
    place = list(xyz)
    place[axis] = lax.rem(place[axis] + by, 4)
    return tuple(place)


def signal(target):
    pl.semaphore_signal(
        pltpu.get_barrier_semaphore(), inc=1, device_id=target, device_id_type=MESH
    )


def remote(src, dst, send, recv, target):
    return pltpu.make_async_remote_copy(
        src_ref=src,
        dst_ref=dst,
        send_sem=send,
        recv_sem=recv,
        device_id=target,
        device_id_type=MESH,
    )


def item_sizes(assignment, image_class, caption_length, xyz, core):
    side = xyz[0] // 2
    group = ((lax.rem(xyz[0], 2) * 2 + xyz[2] // 2) * 4 + xyz[1]) * 2 + core
    chosen = assignment[0, group]
    kept = jnp.where(side == 0, chosen, 1 - chosen)
    images = jnp.where(image_class[0, group, kept] == 1, LARGE_PATCHES, SMALL_PATCHES)
    return side, kept, images, caption_length[0, group, kept]


def valid_of(index, images, captions):
    ok = (index < images) | ((index >= SLOT) & (index < SLOT + captions)) | (index == CLS)
    return ok


class Loads:
    def __init__(self, sem):
        self.sem, self.copies, self.count = sem, {}, 0

    def start(self, name, *pairs):
        self.copies[name] = []
        for src, dst in pairs:
            copy = pltpu.make_async_copy(src, dst, self.sem.at[self.count])
            self.count += 1
            copy.start()
            self.copies[name].append(copy)

    def __call__(self, name):
        for copy in self.copies[name]:
            copy.wait()


def stats(v):
    mean = jnp.mean(v, axis=-1, keepdims=True)
    center = v - mean
    var = jnp.mean(center * center, axis=-1, keepdims=True)
    return center, lax.rsqrt(var + EPS)


GELU_A = 0.7978845608028654
GELU_B = 0.044715


def gelu_both(u):
    u2 = u * u
    t = jnp.tanh(u * (GELU_A + (GELU_A * GELU_B) * u2))
    half = 0.5 + 0.5 * t
    slope = half + (0.5 * u) * (1.0 - t * t) * (GELU_A + (3 * GELU_A * GELU_B) * u2)
    return u * half, slope


NORM_ROWS = 176
QUERY_ROWS = 352


def forward_kernel(
    assignment, image_class, caption_length,
    states, proj_w, qkv_w, out_w, up_w, down_w,
    cls, proj_b, attn_gain, attn_shift, query_b, value_b, out_b, mlp_gain, mlp_shift, up_b, down_b,
    layer_out, raw_o, xh1_o, a1_o, q_o, k_o, v_o, st_o, o_o, xh2_o, a2_o, g_o, gp_o,
    states_s, sent, raw, pw, wqkv, wo, wup, wdn, x, xh1, a1, q, k, v, st, o, h, xh2, a2, g, gp, lsem, osem, xsem,
):
    xyz, core = coords()
    partner = device(along(xyz, 0, 2), core)
    side, kept, images, captions = item_sizes(assignment, image_class, caption_length, xyz, core)
    load = Loads(lsem)
    load.start("states", (states.at[0, 0], states_s))
    load.start("pw", (proj_w, pw))
    load.start("wqkv", (qkv_w, wqkv))
    load.start("wo", (out_w, wo))
    load.start("wup", (up_w, wup))
    load.start("wdn", (down_w, wdn))
    signal(partner)
    pl.semaphore_wait(pltpu.get_barrier_semaphore(), 1)
    load("states")
    sent[...] = jnp.where(kept == 0, states_s[1], states_s[0])
    exchange = remote(sent, raw.at[side], xsem.at[0], xsem.at[1], partner)
    exchange.start()
    raw[side] = jnp.where(kept == 0, states_s[0], states_s[1])

    stores = []

    def put(src, dst):
        copy = pltpu.make_async_copy(src, dst, osem.at[len(stores)])
        copy.start()
        stores.append(copy)

    load("pw")
    row = lax.broadcasted_iota(jnp.int32, (NR, 1), 0)
    valid_col = valid_of(row, images, captions).astype(f32)
    key_row = lax.broadcasted_iota(jnp.int32, (1, NR), 1)
    key_bias = jnp.where(valid_of(key_row, images, captions), 0.0, MASKED)
    gain1, shift1 = row_of(attn_gain), row_of(attn_shift)
    query_bias, value_bias = row_of(query_b), row_of(value_b)
    lane = lax.broadcasted_iota(jnp.int32, (QUERY_ROWS, 128), 1)

    def normed(values, rows, gain, shift, xh_ref, a_ref, stat_lane):
        center, scale = stats(values)
        xh = center * scale
        xh_ref[rows, :] = xh.astype(bf16)
        a_ref[rows, :] = (xh * gain + shift).astype(bf16)
        lanes = lax.broadcasted_iota(jnp.int32, (values.shape[0], 128), 1)
        st[rows, :] = jnp.where(lanes == stat_lane, scale, st[rows, :])

    def qkv(first, count):
        rows = pl.ds(first, count)
        a = a1[rows, :]
        for part, ref in enumerate((q, k, v)):
            for j in range(3):
                cols = slice(j * 256, j * 256 + 256)
                m = dot(a, wqkv[:, part * D + j * 256 : part * D + j * 256 + 256])
                if part == 0:
                    m = (m + query_bias[:, cols]) * 0.125
                if part == 2:
                    m = m + value_bias[:, cols]
                ref[rows, cols] = m.astype(bf16)

    st[...] = jnp.zeros_like(st)

    def one_side(which):
        first = pl.multiple_of(which * SLOT, 16)
        limit = jnp.where(which == 0, images, captions)
        keep = lax.broadcasted_iota(jnp.int32, (SLOT, 1), 0) < limit
        bias = jnp.where(which == 0, proj_b[0:1, :].astype(f32), proj_b[1:2, :].astype(f32))
        for j in range(3):
            cols = slice(j * 256, j * 256 + 256)
            p = (dot(raw[which], pw[which, :, cols]) + bias[:, cols]).astype(bf16)
            x[pl.ds(first, SLOT), cols] = jnp.where(keep, p, 0).astype(bf16)

        def norm_step(i):
            rows = pl.ds(pl.multiple_of(first + i * 112, 16), 112)
            normed(x[rows, :].astype(f32), rows, gain1, shift1, xh1, a1, 12)

        loop(3, norm_step)
        qkv(first, SLOT)

    x[CLS:NR, :] = jnp.where(
        lax.broadcasted_iota(jnp.int32, (NR - CLS, 1), 0) == 0, row_of(cls), 0.0
    ).astype(bf16)
    normed(x[CLS:NR, :].astype(f32), slice(CLS, NR), gain1, shift1, xh1, a1, 12)
    load("wqkv")
    qkv(CLS, NR - CLS)
    one_side(side)
    exchange.wait()
    one_side(1 - side)
    put(raw, raw_o)
    put(xh1, xh1_o)
    put(a1, a1_o)
    put(q, q_o)
    put(k, k_o)
    put(v, v_o)

    def attend(i):
        p = i // (NR // QUERY_ROWS)
        rows, cols = span(lax.rem(i, NR // QUERY_ROWS), QUERY_ROWS), span(p, 128)
        queries, keys, values = q[rows, cols], k[:, cols], v[:, cols]
        both, kept_stats = [], st[rows, :]
        for head in range(2):
            s = dot(jnp.where(lane // 64 == head, queries, 0).astype(bf16), keys, NT) + key_bias
            peak = jnp.max(s, axis=-1, keepdims=True)
            e = jnp.exp(s - peak)
            total = jnp.sum(e, axis=-1, keepdims=True)
            both.append(dot(e.astype(bf16), values) * (1.0 / total))
            kept_stats = jnp.where(lane == 2 * p + head, peak + jnp.log(total), kept_stats)
        o[rows, cols] = jnp.where(lane < 64, both[0], both[1]).astype(bf16)
        st[rows, :] = kept_stats

    loop(6 * (NR // QUERY_ROWS), attend)
    put(o, o_o)
    load("wo")
    out_bias = row_of(out_b)
    for j in range(3):
        cols = slice(j * 256, j * 256 + 256)
        h[:, cols] = x[:, cols].astype(f32) + dot(o[...], wo[:, cols]) + out_bias[:, cols]
    gain2, shift2 = row_of(mlp_gain), row_of(mlp_shift)

    def norm_two(i):
        rows = pl.ds(pl.multiple_of(i * 176, 16), 176)
        normed(h[rows, :], rows, gain2, shift2, xh2, a2, 13)

    loop(NR // 176, norm_two)
    put(st, st_o)
    put(xh2, xh2_o)
    put(a2, a2_o)
    load("wup")
    up_bias = row_of(up_b)
    for j in range(12):
        cols = slice(j * 256, j * 256 + 256)
        u = dot(a2[...], wup[:, cols]) + up_bias[:, cols]
        value, slope = gelu_both(u)
        g[:, cols] = value.astype(bf16)
        gp[:, cols] = slope.astype(bf16)
    put(g, g_o)
    put(gp, gp_o)
    load("wdn")
    down_bias = row_of(down_b)
    for j in range(3):
        cols = slice(j * 256, j * 256 + 256)
        y = (h[:, cols] + dot(g[...], wdn[:, cols]) + down_bias[:, cols]) * valid_col
        y = jnp.where(row == 0, y[CLS : CLS + 1, :], pltpu.roll(y, 1, 0))
        layer_out[0, 0, :, cols] = y[:SEQ].astype(bf16)
    for copy in stores:
        copy.wait()


CHUNK = 1536
HALF = 768
Q1 = 192
Q2 = 48
CHUNKS = 7


class Comm:
    def __init__(self, g, hx, r1, s1, r2, r3, f1, ssem, rsem, lsem, tiny, tbuf, tsem, outs):
        self.g, self.hx, self.r1, self.s1, self.r2, self.r3, self.f1 = g, hx, r1, s1, r2, r3, f1
        self.ssem, self.rsem, self.lsem = ssem, rsem, lsem
        self.tiny, self.tbuf, self.tsem, self.outs = tiny, tbuf, tsem, outs
        self.xyz, self.core = coords()

    def partners(self):
        yield device(self.xyz, 1 - self.core)
        for axis in range(3):
            for by in (1, 2, 3):
                yield device(along(self.xyz, axis, by), self.core)

    def greet(self):
        for target in self.partners():
            signal(target)
        pl.semaphore_wait(pltpu.get_barrier_semaphore(), 10)

    def copy(self, src, dst, i, j, target):
        return remote(src, dst, self.ssem.at[i, j], self.rsem.at[i, j], target)

    def copies(self, i, stage, k=0):
        core, xyz = self.core, self.xyz
        cols = pl.ds(k * 256, 256)
        if stage == 0:
            src = self.g.at[i % 2, pl.ds((1 - core) * HALF, HALF)]
            return [self.copy(src, self.hx.at[i], i, 0, device(xyz, 1 - core))]
        if stage == 6:
            part = self.outs[i].at[pl.ds(core * HALF, HALF), cols]
            return [self.copy(part, part, i, 46 + k, device(xyz, 1 - core))]
        result = []
        axis = (k + {1: 0, 2: 1, 3: 2, 4: 1, 5: 0}[stage]) % 3
        for by in (2, 1, 3):
            j = 1 + (stage - 1) * 9 + k * 3 + by - 1
            place = along(xyz, axis, by)
            if stage == 1:
                src = self.hx.at[i, pl.ds(place[axis] * Q1, Q1), cols]
                dst = self.r1.at[i, k, by - 1]
            if stage == 2:
                src = self.s1.at[i, k, pl.ds(place[axis] * Q2, Q2)]
                dst = self.r2.at[i, k, by - 1]
            if stage == 3:
                src = dst = self.r3.at[i, k, xyz[axis]]
            if stage == 4:
                src = dst = self.f1.at[i, k, pl.ds(xyz[axis] * Q2, Q2)]
            if stage == 5:
                src = self.f1.at[i, k]
                dst = self.outs[i].at[pl.ds(core * HALF + xyz[axis] * Q1, Q1), cols]
            result.append(self.copy(src, dst, i, j, device(place, core)))
        return result

    def start(self, i, stage, k=0):
        for copy in self.copies(i, stage, k):
            copy.start()

    def wait(self, i, stage, k=0):
        for copy in self.copies(i, stage, k):
            copy.wait()

    def add_halves(self, i):
        def body(j):
            rows = span(j, 64)
            own = self.g[i % 2, pl.ds(pl.multiple_of(self.core * HALF + j * 64, 64), 64), :]
            self.hx[i, rows, :] = (own.astype(f32) + self.hx[i, rows, :].astype(f32)).astype(bf16)

        loop(HALF // 64, body)

    def add(self, i, stage, k):
        place = self.xyz[(k + stage - 1) % 3]
        if stage == 1:

            def body(j):
                rows = span(j, 96)
                first = pl.multiple_of(place * Q1 + j * 96, 96)
                v = self.hx[i, pl.ds(first, 96), pl.ds(k * 256, 256)].astype(f32)
                for d in range(3):
                    v = v + self.r1[i, k, d, rows, :].astype(f32)
                self.s1[i, k, rows, :] = v.astype(bf16)

            loop(Q1 // 96, body)
        if stage == 2:
            v = self.s1[i, k, pl.ds(pl.multiple_of(place * Q2, Q2), Q2), :].astype(f32)
            for d in range(3):
                v = v + self.r2[i, k, d].astype(f32)
            self.r3[i, k, self.xyz[(k + 2) % 3]] = v.astype(bf16)
        if stage == 3:
            v = self.r3[i, k, 0].astype(f32)
            for d in range(1, 4):
                v = v + self.r3[i, k, d].astype(f32)
            mine = self.xyz[(k + 1) % 3]
            self.f1[i, k, pl.ds(pl.multiple_of(mine * Q2, Q2), Q2), :] = v.astype(bf16)

    def place(self, i, k):
        first = self.core * HALF + self.xyz[k] * Q1
        dst = self.outs[i].at[pl.ds(first, Q1), pl.ds(k * 256, 256)]
        return pltpu.make_async_copy(self.f1.at[i, k], dst, self.lsem.at[i, k])

    def stage(self, i, stage):
        if stage == 0:
            self.start(i, 0)
        elif stage == 1:
            self.wait(i, 0)
            self.add_halves(i)
            for k in range(3):
                self.start(i, 1, k)
        else:
            for k in range(3):
                self.wait(i, stage - 1, k)
                if stage <= 4:
                    self.add(i, stage - 1, k)
                if stage == 5:
                    self.place(i, k).start()
                if stage == 6:
                    self.place(i, k).wait()
                if stage <= 6:
                    self.start(i, stage, k)


    def tiny_copies(self, step):
        core, xyz = self.core, self.xyz
        part = self.tbuf.at[step, core if step == 0 else xyz[step - 1]]
        pairs = [(device(xyz, 1 - core), 0)]
        if step > 0:
            pairs = [(device(along(xyz, step - 1, by), core), by - 1) for by in (2, 1, 3)]
        return [
            remote(part, part, self.tsem.at[0, step, j], self.tsem.at[1, step, j], target)
            for target, j in pairs
        ]

    def tiny_stage(self, step):
        if step == 0:
            self.tbuf[0, self.core] = self.tiny[...]
        else:
            for copy in self.tiny_copies(step - 1):
                copy.wait()
            v = self.tbuf[step - 1, 0]
            for d in range(1, 2 if step == 1 else 4):
                v = v + self.tbuf[step - 1, d]
            if step < 4:
                self.tbuf[step, self.xyz[step - 1]] = v
            else:
                self.tiny[...] = v
        if step < 4:
            for copy in self.tiny_copies(step):
                copy.start()


COMM_SCRATCH = [
    pltpu.VMEM((2, CHUNK, D), bf16),
    pltpu.VMEM((CHUNKS, HALF, D), bf16),
    pltpu.VMEM((CHUNKS, 3, 3, Q1, 256), bf16),
    pltpu.VMEM((CHUNKS, 3, Q1, 256), bf16),
    pltpu.VMEM((CHUNKS, 3, 3, Q2, 256), bf16),
    pltpu.VMEM((CHUNKS, 3, 4, Q2, 256), bf16),
    pltpu.VMEM((CHUNKS, 3, Q1, 256), bf16),
    pltpu.SemaphoreType.DMA((CHUNKS, 49)),
    pltpu.SemaphoreType.DMA((CHUNKS, 49)),
    pltpu.SemaphoreType.DMA((CHUNKS, 3)),
    pltpu.VMEM((16, D), f32),
    pltpu.VMEM((4, 4, 16, D), f32),
    pltpu.SemaphoreType.DMA((2, 4, 3)),
]

D0, D1, U0, U1, OQ, KV, PR = range(CHUNKS)
SCHEDULE = {
    "D0": [(D0, 0)],
    "D1": [(D1, 0), (D0, 1)],
    "dU0": [(D1, 1)],
    "U0": [(U0, 0)],
    "dU1": [(U0, 1), (D0, 2)],
    "U1": [(U1, 0), (D1, 2)],
    "dA2": [(U1, 1), (D0, 3), (D1, 3)],
    "N2": [(D0, 4), (D1, 4)],
    "dO": [(U0, 2), (D0, 5), (D1, 5)],
    ("att", 0): [(U0, 3), (U1, 2)],
    ("att", 1): [(U0, 4), (U1, 3)],
    ("att", 2): [(D0, 6), (U0, 5), (U1, 4)],
    ("att", 3): [(D1, 6), (U1, 5)],
    ("att", 4): [(U0, 6)],
    ("att", 5): [(U1, 6)],
    "O": [(OQ, 0)],
    "KV": [(KV, 0), (OQ, 1)],
    "dA1": [(KV, 1), (OQ, 2)],
    "N1": [(OQ, 3), (KV, 2)],
    "P": [(PR, 0), "t0", (OQ, 4), (KV, 3)],
    "back": [(PR, 1), "t1", (KV, 4), (OQ, 5)],
    "end": [
        (PR, 2), "t2", (KV, 5), (PR, 3), "t3", (OQ, 6), (PR, 4), "t4", (KV, 6), (PR, 5), (PR, 6),
        (D0, 7), (D1, 7), (U0, 7), (U1, 7), (OQ, 7), (KV, 7), (PR, 7),
    ],
}

KEY_ROWS = 352
WO = 3 * D
WP = 4 * D


def backward_kernel(
    assignment, image_class, caption_length,
    cotangent, raw_i, xh1_i, a1_i, q_i, k_i, v_i, st_i, o_i, xh2_i, a2_i, g_i, gp_i,
    proj_w, qkv_w, out_w, up_w, down_w, attn_gain, mlp_gain,
    o0, o1, o2, o3, o4, o5, o6, tiny_o, back_o,
    W, GA, GB, dy, a2, xh2, a1, xh1, raw, stc, stt, da, dh, dp, acc, dq_s, sg, lsem, bsem, *comm_scratch,
):
    comm = Comm(*comm_scratch, outs=(o0, o1, o2, o3, o4, o5, o6))
    xyz, core = comm.xyz, comm.core
    tiny = comm.tiny
    partner = device(along(xyz, 0, 2), core)
    side, _, images, captions = item_sizes(assignment, image_class, caption_length, xyz, core)

    def hook(name):
        for due in SCHEDULE.get(name, ()):
            if isinstance(due, str):
                comm.tiny_stage(int(due[1]))
            else:
                comm.stage(*due)

    load = Loads(lsem)
    load.start("g", *[(g_i.at[:, b * D : b * D + D], GA.at[b]) for b in range(4)])
    load.start("wd", (down_w, W.at[0:FF]))
    load.start("gp", *[(gp_i.at[:, b * D : b * D + D], GB.at[b]) for b in range(4)])
    load.start("a2", (a2_i, a2))
    load.start("wu", *[(up_w.at[:, b * D : b * D + D], W.at[FF + b * D : FF + b * D + D]) for b in range(4)])
    load.start("st", (st_i, stc))
    load.start("xh2", (xh2_i, xh2))
    comm.greet()

    row = lax.broadcasted_iota(jnp.int32, (NR, 1), 0)
    valid_col = valid_of(row, images, captions)
    key_bias = jnp.where(valid_col, 0.0, MASKED)
    for j in range(3):
        cols = slice(j * 256, j * 256 + 256)
        da[0:SEQ, cols] = cotangent[0, 0, :, cols].astype(f32)
        v = da[:, cols]
        v = jnp.where(row == CLS, v[0:1, :], pltpu.roll(v, NR - 1, 0))
        dy[:, cols] = jnp.where(valid_col, v, 0.0).astype(bf16)

    ones = jnp.ones((16, NR), bf16)

    def column_sums(at, value):
        tiny[at : at + 1, :] = dot(ones[:, : value.shape[0]], value)[0:1, :]

    def emit(i, first, j, value):
        comm.g[i % 2, span(j, 256, first), :] = value.astype(bf16)

    def down_grad(i, b, first):
        loop(3, lambda j: emit(i, first, j, dot(GA[b, :, span(j, 256)], dy[...], TN)))

    load("g")
    down_grad(D0, 0, 0)
    down_grad(D0, 1, D)
    hook("D0")
    down_grad(D1, 2, 0)
    down_grad(D1, 3, D)
    hook("D1")
    load.start("qkvo", (q_i, GA.at[0]), (k_i, GA.at[1]), (v_i, GA.at[2]), (o_i, GA.at[3]))
    load.start("a1", (a1_i, a1))
    load.start("xh1", (xh1_i, xh1))
    load.start("raw", (raw_i, raw))
    column_sums(14, dy[...])

    def gate_grad(b):
        def body(j):
            cols = span(j, 256)
            v = dot(dy[...], W[span(j, 256, b * D), :], NT)
            GB[b, :, cols] = (v * GB[b, :, cols].astype(f32)).astype(bf16)

        loop(3, body)

    def up_grad(i, b, first):
        loop(3, lambda j: emit(i, first, j, dot(a2[:, span(j, 256)], GB[b], TN)))

    load("wd")
    load("gp")
    gate_grad(0)
    gate_grad(1)
    hook("dU0")
    load("a2")
    up_grad(U0, 0, 0)
    up_grad(U0, 1, D)
    hook("U0")
    gate_grad(2)
    gate_grad(3)
    hook("dU1")
    load.start("wqkv", *[(qkv_w.at[:, b * D : b * D + D], W.at[b * D : b * D + D]) for b in range(3)])
    load.start("wo", (out_w, W.at[WO : WO + D]))
    up_grad(U1, 2, 0)
    up_grad(U1, 3, D)
    hook("U1")
    for b in range(4):
        column_sums(10 + b, GB[b])

    def input_grad(first, blocks):
        def body(j):
            v = dot(GB[0], W[span(j, 256, first), :], NT)
            for b in range(1, blocks):
                v = v + dot(GB[b], W[span(j, 256, first + b * D), :], NT)
            da[:, span(j, 256)] = v

        loop(3, body)

    load("wu")
    input_grad(FF, 4)
    load.start("pw", (proj_w.at[0], W.at[WP : WP + D]), (proj_w.at[1], W.at[WP + D : WP + 2 * D]))
    hook("dA2")

    def norm_back(gain_ref, xh_ref, stat_lane, add_to, at):
        gain = row_of(gain_ref)
        acc[...] = jnp.zeros_like(acc)

        def body(i):
            rows = span(i, NORM_ROWS)
            d, xh, scale = da[rows, :], xh_ref[rows, :].astype(f32), stc[rows, stat_lane : stat_lane + 1]
            gg = d * gain
            m1 = jnp.mean(gg, axis=-1, keepdims=True)
            m2 = jnp.mean(gg * xh, axis=-1, keepdims=True)
            dh[rows, :] = add_to(rows) + scale * (gg - m1 - xh * m2)
            acc[0] += jnp.sum((d * xh).reshape(NORM_ROWS // 8, 8, D), axis=0)
            acc[1] += jnp.sum(d.reshape(NORM_ROWS // 8, 8, D), axis=0)

        loop(NR // NORM_ROWS, body)
        tiny[at : at + 1, :] = jnp.sum(acc[0], axis=0, keepdims=True)
        tiny[at + 1 : at + 2, :] = jnp.sum(acc[1], axis=0, keepdims=True)

    load("xh2")
    load("st")
    norm_back(mlp_gain, xh2, 13, lambda rows: dy[rows, :].astype(f32), 8)
    hook("N2")
    dy[...] = dh[...].astype(bf16)
    load("qkvo")
    queries, keys, values, attended = (GA.at[b] for b in range(4))
    d_q, d_k, d_v, d_o = (GB.at[b] for b in range(4))
    loop(3, lambda j: emit(OQ, 0, j, dot(attended[:, span(j, 256)], dy[...], TN)))
    column_sums(7, dy[...])
    load("wo")

    def attended_grad(j):
        d_o[:, span(j, 256)] = dot(dy[...], W[span(j, 256, WO), :], NT).astype(bf16)

    loop(3, attended_grad)
    hook("dO")
    stt[...] = jnp.transpose(stc[...])
    lane = lax.broadcasted_iota(jnp.int32, (NR, 128), 1)
    head_of = lax.broadcasted_iota(jnp.int32, (16, 128), 1) // 64
    select = (head_of == lax.broadcasted_iota(jnp.int32, (16, 128), 0)).astype(bf16)

    def attend_back(p):
        cols = span(p, 128)
        qq, do = queries[:, cols], d_o[:, cols]
        product = do.astype(f32) * attended[:, cols].astype(f32)
        high = product.astype(bf16)
        low = (product - high.astype(f32)).astype(bf16)
        delta = dot(select, high, NT) + dot(select, low, NT)
        q_of = [jnp.where(lane // 64 == head, qq, 0).astype(bf16) for head in range(2)]
        do_of = [jnp.where(lane // 64 == head, do, 0).astype(bf16) for head in range(2)]
        for kb in range(NR // KEY_ROWS):
            rows = slice(kb * KEY_ROWS, (kb + 1) * KEY_ROWS)
            kk, vv = keys[rows, cols], values[rows, cols]
            dk = dv = None
            for head in range(2):
                s = dot(kk, q_of[head], NT) + key_bias[rows] - stt[pl.ds(2 * p + head, 1), :]
                pr = jnp.exp(s)
                dpr = dot(vv, do_of[head], NT)
                ds = (pr * (dpr - delta[head : head + 1, :])).astype(bf16)
                dv_part, dk_part = dot(pr.astype(bf16), do_of[head]), dot(ds, q_of[head])
                k_of = jnp.where(lane[:KEY_ROWS] // 64 == head, kk, 0).astype(bf16)
                dq = dot(ds, k_of, TN)
                dk, dv = (dk_part, dv_part) if dk is None else (dk + dk_part, dv + dv_part)
                if kb == 0 and head == 0:
                    dq_s[...] = dq
                else:
                    dq_s[...] += dq
            d_k[rows, cols] = dk.astype(bf16)
            d_v[rows, cols] = dv.astype(bf16)
        d_q[:, cols] = (dq_s[...].astype(bf16).astype(f32) * 0.125).astype(bf16)
        for at in range(6):

            @pl.when(p == at)
            def _():
                hook(("att", at))

    loop(6, attend_back)
    load("a1")
    loop(3, lambda j: emit(OQ, D, j, dot(a1[:, span(j, 256)], d_q[...], TN)))
    hook("O")
    loop(3, lambda j: emit(KV, 0, j, dot(a1[:, span(j, 256)], d_k[...], TN)))
    loop(3, lambda j: emit(KV, D, j, dot(a1[:, span(j, 256)], d_v[...], TN)))
    hook("KV")
    column_sums(5, d_q[...])
    column_sums(6, d_v[...])
    load("wqkv")
    input_grad(0, 3)
    hook("dA1")
    load("xh1")
    norm_back(attn_gain, xh1, 12, lambda rows: dh[rows, :], 3)
    hook("N1")
    tiny[0:1, :] = dh[CLS : CLS + 1, :]
    tiny[15:16, :] = jnp.zeros((1, D), f32)
    load("raw")
    for s in range(2):
        dp[s] = dh[s * SLOT : (s + 1) * SLOT, :].astype(bf16)
        loop(3, lambda j: emit(PR, s * D, j, dot(raw[s, :, span(j, 256)], dp[s], TN)))
        column_sums(1 + s, dp[s])
    hook("P")
    load("pw")

    def states_back(which, slot):
        def body(j):
            v = dot(dp[which], W[span(j, 256, WP + which * D), :], NT)
            sg[slot, :, span(j, 256)] = v.astype(bf16)

        loop(3, body)

    states_back(1 - side, 1)
    returned = remote(sg.at[1], back_o.at[1], bsem.at[0], bsem.at[1], partner)
    returned.start()
    states_back(side, 0)
    own = pltpu.make_async_copy(sg.at[0], back_o.at[0], bsem.at[2])
    own.start()
    hook("back")
    hook("end")
    final = pltpu.make_async_copy(tiny, tiny_o, bsem.at[3])
    final.start()
    final.wait()
    own.wait()
    returned.wait()


PIECE = 768


def unpack_kernel(
    assignment, back, c0, c1, c2, c3, c4, c5, c6, tiny_i,
    states_grad, cls, proj_w, proj_b, attn_gain, attn_shift, qkv_w, query_b, value_b, out_w, out_b,
    mlp_gain, mlp_shift, up_w, up_b, down_w, down_b,
    src, dst, tiny, small, isem, osem, bsem, msem,
):
    xyz, core = coords()
    side = xyz[0] // 2
    group = ((lax.rem(xyz[0], 2) * 2 + xyz[2] // 2) * 4 + xyz[1]) * 2 + core
    chosen = assignment[0, group]
    kept = jnp.where(side == 0, chosen, 1 - chosen)
    moves = [
        pltpu.make_async_copy(back.at[0], states_grad.at[0, 0, kept], bsem.at[0]),
        pltpu.make_async_copy(back.at[1], states_grad.at[0, 0, 1 - kept], bsem.at[1]),
        pltpu.make_async_copy(tiny_i, tiny, bsem.at[2]),
    ]
    for move in moves:
        move.start()
    blocks = []
    for b, chunk in enumerate((c0, c0, c1, c1)):
        blocks.append((chunk, b % 2, down_w.at[b * D : b * D + D]))
    for b, chunk in enumerate((c2, c2, c3, c3)):
        blocks.append((chunk, b % 2, up_w.at[:, b * D : b * D + D]))
    blocks.append((c4, 0, out_w))
    for b, (chunk, at) in enumerate(((c4, 1), (c5, 0), (c5, 1))):
        blocks.append((chunk, at, qkv_w.at[:, b * D : b * D + D]))
    for b in range(2):
        blocks.append((c6, b, proj_w.at[b]))
    n = len(blocks)
    depth = 4

    def read(i):
        chunk, at, _ = blocks[i]
        return pltpu.make_async_copy(chunk.at[at * D : at * D + D], src.at[i % depth], isem.at[i % depth])

    def write(i):
        return pltpu.make_async_copy(dst.at[i % depth], blocks[i][2], osem.at[i % depth])

    for i in range(depth):
        read(i).start()
    for i in range(n):
        read(i).wait()
        if i >= depth:
            write(i - depth).wait()

        def body(j):
            dst[i % depth, span(j, 64), :] = src[i % depth, span(j, 64), :].astype(f32)

        loop(D // 64, body)
        write(i).start()
        if i + depth < n:
            read(i + depth).start()
    moves[2].wait()
    for ref, at in ((cls, 0), (attn_gain, 3), (attn_shift, 4), (query_b, 5), (value_b, 6), (out_b, 7), (mlp_gain, 8), (mlp_shift, 9), (down_b, 14)):
        ref[...] = tiny[at : at + 1, :].reshape(D)
    proj_b[...] = tiny[1:3, :]
    for b in range(4):
        up_b[pl.ds(b * D, D)] = tiny[10 + b : 11 + b, :].reshape(D)
    for i in range(n - depth, n):
        write(i).wait()
    moves[0].wait()
    moves[1].wait()


def shape(*dims, dtype=bf16):
    return jax.ShapeDtypeStruct(dims, dtype)


def scratch(*dims, dtype=bf16):
    return pltpu.VMEM(dims, dtype)


ANY = pl.BlockSpec(memory_space=pl.ANY)
VMEM = pl.BlockSpec(memory_space=pltpu.VMEM)
SMEM = pl.BlockSpec(memory_space=pltpu.SMEM)
DMA = pltpu.SemaphoreType.DMA
ITEM = (NR, D)


def per_device(
    side_states, assignment, image_class, caption_length, cls_token, proj_weight, proj_bias,
    attn_gain, attn_shift, qkv_weight, query_bias, value_bias, out_weight, out_bias,
    mlp_gain, mlp_shift, up_weight, up_bias, down_weight, down_bias, out_cotangent,
):
    sizes = (assignment, image_class, caption_length)
    layer_out, raw, xh1, a1, q, k, v, st, o, xh2, a2, g, gp = pl.pallas_call(
        forward_kernel,
        out_shape=[
            shape(1, 1, SEQ, D), shape(2, SLOT, D), shape(*ITEM), shape(*ITEM), shape(*ITEM), shape(*ITEM),
            shape(*ITEM), shape(NR, 128, dtype=f32), shape(*ITEM), shape(*ITEM), shape(*ITEM),
            shape(NR, FF), shape(NR, FF),
        ],
        in_specs=[SMEM] * 3 + [ANY] * 6 + [VMEM] * 11,
        out_specs=[VMEM] + [ANY] * 12,
        scratch_shapes=[
            scratch(2, SLOT, D), scratch(SLOT, D), scratch(2, SLOT, D),
            scratch(2, D, D), scratch(D, 3 * D), scratch(D, D), scratch(D, FF), scratch(FF, D),
            scratch(*ITEM), scratch(*ITEM), scratch(*ITEM), scratch(*ITEM), scratch(*ITEM), scratch(*ITEM),
            scratch(NR, 128, dtype=f32), scratch(*ITEM), scratch(*ITEM, dtype=f32), scratch(*ITEM), scratch(*ITEM),
            scratch(NR, FF), scratch(NR, FF), DMA((6,)), DMA((12,)), DMA((2,)),
        ],
        compiler_params=pltpu.CompilerParams(collective_id=0, has_side_effects=True, vmem_limit_bytes=62 * MIB),
        name="forward",
    )(
        *sizes, side_states, proj_weight, qkv_weight, out_weight, up_weight, down_weight,
        cls_token, proj_bias, attn_gain, attn_shift, query_bias, value_bias, out_bias,
        mlp_gain, mlp_shift, up_bias, down_bias,
    )
    *chunks, tiny, back = pl.pallas_call(
        backward_kernel,
        out_shape=[shape(CHUNK, D)] * CHUNKS + [shape(16, D, dtype=f32), shape(2, SLOT, D)],
        in_specs=[SMEM] * 3 + [VMEM] + [ANY] * 17 + [VMEM] * 2,
        out_specs=[ANY] * (CHUNKS + 2),
        scratch_shapes=[
            scratch(8 * D, D), scratch(4, *ITEM), scratch(4, *ITEM),
            scratch(*ITEM), scratch(*ITEM), scratch(*ITEM), scratch(*ITEM), scratch(*ITEM), scratch(2, SLOT, D),
            scratch(NR, 128, dtype=f32), scratch(128, NR, dtype=f32),
            scratch(*ITEM, dtype=f32), scratch(*ITEM, dtype=f32), scratch(2, SLOT, D),
            scratch(2, 8, D, dtype=f32), scratch(NR, 128, dtype=f32), scratch(2, SLOT, D),
            DMA((32,)), DMA((4,)), *COMM_SCRATCH,
        ],
        compiler_params=pltpu.CompilerParams(collective_id=1, has_side_effects=True, vmem_limit_bytes=63 * MIB),
        name="backward",
    )(
        *sizes, out_cotangent, raw, xh1, a1, q, k, v, st, o, xh2, a2, g, gp,
        proj_weight, qkv_weight, out_weight, up_weight, down_weight, attn_gain, mlp_gain,
    )
    vector = shape(D, dtype=f32)
    grads = pl.pallas_call(
        unpack_kernel,
        out_shape=[
            shape(1, 1, 2, SLOT, D), vector, shape(2, D, D, dtype=f32), shape(2, D, dtype=f32), vector, vector,
            shape(D, 3 * D, dtype=f32), vector, vector, shape(D, D, dtype=f32), vector, vector, vector,
            shape(D, FF, dtype=f32), shape(FF, dtype=f32), shape(FF, D, dtype=f32), vector,
        ],
        in_specs=[SMEM] + [ANY] * (CHUNKS + 2),
        out_specs=[ANY, VMEM, ANY, VMEM, VMEM, VMEM, ANY, VMEM, VMEM, ANY, VMEM, VMEM, VMEM, ANY, VMEM, ANY, VMEM],
        scratch_shapes=[
            scratch(4, PIECE, D), scratch(4, PIECE, D, dtype=f32), scratch(16, D, dtype=f32), scratch(8, D, dtype=f32),
            DMA((4,)), DMA((4,)), DMA((3,)), DMA((1,)),
        ],
        compiler_params=pltpu.CompilerParams(vmem_limit_bytes=62 * MIB),
        name="unpack",
    )(assignment, back, *chunks, tiny)
    return (layer_out, *grads)


def solution(mesh):
    weights = (P(),) * 16
    return jax.shard_map(
        per_device,
        mesh=mesh,
        in_specs=(P("items", "tower"), P("items"), P("items"), P("items"), *weights, P("items", "tower")),
        out_specs=(P("items", "tower"), P("items", "tower"), *weights),
        check_vma=False,
    )
```

```python
import jax
import jax.numpy as jnp
from jax import lax
from jax.experimental import pallas as pl
from jax.experimental.pallas import tpu as pltpu
from jax.sharding import PartitionSpec as P

bf16 = jnp.bfloat16
f32 = jnp.float32
MESH = pl.DeviceIdType.MESH
D = 768
FF = 3072
SLOT = 336
SEQ = 673
SMALL_PATCHES = 197
LARGE_PATCHES = 325
NR = 704
CLS = 2 * SLOT
EPS = 1e-5
MASKED = -1e30
MIB = 2**20

NN = (((1,), (0,)), ((), ()))
NT = (((1,), (1,)), ((), ()))
TN = (((0,), (0,)), ((), ()))


def dot(a, b, dims=NN):
    return lax.dot_general(a, b, dims, preferred_element_type=f32)


def loop(n, body, start=0):
    def step(i, carry):
        body(i)
        return carry

    lax.fori_loop(start, n, step, 0)


def span(i, n, base=0):
    return pl.ds(pl.multiple_of(base + i * n, n), n)


def row_of(ref):
    return ref[...].astype(f32).reshape(1, ref.shape[0])


def coords():
    items, tower = lax.axis_index("items"), lax.axis_index("tower")
    x, y = tower // 16, lax.rem(tower // 2, 4)
    return (x, y, lax.rem(tower // 8, 2) * 2 + items), lax.rem(tower, 2)


def device(xyz, core):
    x, y, z = xyz
    return lax.rem(z, 2), ((x * 2 + z // 2) * 4 + y) * 2 + core


def along(xyz, axis, by):
    place = list(xyz)
    place[axis] = lax.rem(place[axis] + by, 4)
    return tuple(place)


def signal(target):
    pl.semaphore_signal(
        pltpu.get_barrier_semaphore(), inc=1, device_id=target, device_id_type=MESH
    )


def remote(src, dst, send, recv, target):
    return pltpu.make_async_remote_copy(
        src_ref=src,
        dst_ref=dst,
        send_sem=send,
        recv_sem=recv,
        device_id=target,
        device_id_type=MESH,
    )


def item_sizes(assignment, image_class, caption_length, xyz, core):
    side = xyz[0] // 2
    group = ((lax.rem(xyz[0], 2) * 2 + xyz[2] // 2) * 4 + xyz[1]) * 2 + core
    chosen = assignment[0, group]
    kept = jnp.where(side == 0, chosen, 1 - chosen)
    images = jnp.where(image_class[0, kept, group] == 1, LARGE_PATCHES, SMALL_PATCHES)
    return side, kept, images, caption_length[0, kept, group]


def valid_of(index, images, captions):
    ok = (index < images) | ((index >= SLOT) & (index < SLOT + captions)) | (index == CLS)
    return ok


class Loads:
    def __init__(self, sem):
        self.sem, self.copies, self.count = sem, {}, 0

    def start(self, name, *pairs):
        self.copies[name] = []
        for src, dst in pairs:
            copy = pltpu.make_async_copy(src, dst, self.sem.at[self.count])
            self.count += 1
            copy.start()
            self.copies[name].append(copy)

    def __call__(self, name):
        for copy in self.copies[name]:
            copy.wait()


def stats(v):
    mean = jnp.mean(v, axis=-1, keepdims=True)
    center = v - mean
    var = jnp.mean(center * center, axis=-1, keepdims=True)
    return center, lax.rsqrt(var + EPS)


GELU_A = 0.7978845608028654
GELU_B = 0.044715


def gelu_both(u):
    u2 = u * u
    t = jnp.tanh(u * (GELU_A + (GELU_A * GELU_B) * u2))
    half = 0.5 + 0.5 * t
    slope = half + (0.5 * u) * (1.0 - t * t) * (GELU_A + (3 * GELU_A * GELU_B) * u2)
    return u * half, slope


NORM_ROWS = 176
QUERY_ROWS = 352


def forward_kernel(
    assignment, image_class, caption_length,
    states, proj_w, qkv_w, out_w, up_w,
    cls, proj_b, attn_gain, attn_shift, query_b, value_b, out_b, mlp_gain, mlp_shift, up_b,
    raw_o, xh1_o, a1_o, q_o, k_o, v_o, st_o, o_o, h_o, xh2_o, a2_o, g_o, gp_o,
    states_s, sent, raw, pw, wqkv, wo, wup, x, xh1, a1, q, k, v, st, o, h, xh2, a2, g, gp, lsem, osem, xsem,
):
    xyz, core = coords()
    partner = device(along(xyz, 0, 2), core)
    side, kept, images, captions = item_sizes(assignment, image_class, caption_length, xyz, core)
    load = Loads(lsem)
    load.start("states", (states.at[0, 0], states_s))
    load.start("pw", (proj_w, pw))
    load.start("wqkv", (qkv_w, wqkv))
    load.start("wo", (out_w, wo))
    load.start("wup", (up_w, wup))
    signal(partner)
    pl.semaphore_wait(pltpu.get_barrier_semaphore(), 1)
    load("states")
    sent[...] = jnp.where(kept == 0, states_s[1], states_s[0])
    exchange = remote(sent, raw.at[side], xsem.at[0], xsem.at[1], partner)
    exchange.start()
    raw[side] = jnp.where(kept == 0, states_s[0], states_s[1])

    stores = []

    def put(src, dst):
        copy = pltpu.make_async_copy(src, dst, osem.at[len(stores)])
        copy.start()
        stores.append(copy)

    load("pw")
    key_row = lax.broadcasted_iota(jnp.int32, (1, NR), 1)
    key_bias = jnp.where(valid_of(key_row, images, captions), 0.0, MASKED)
    gain1, shift1 = row_of(attn_gain), row_of(attn_shift)
    query_bias, value_bias = row_of(query_b), row_of(value_b)
    lane = lax.broadcasted_iota(jnp.int32, (QUERY_ROWS, 128), 1)

    def normed(values, rows, gain, shift, xh_ref, a_ref, stat_lane):
        center, scale = stats(values)
        xh = center * scale
        xh_ref[rows, :] = xh.astype(bf16)
        a_ref[rows, :] = (xh * gain + shift).astype(bf16)
        lanes = lax.broadcasted_iota(jnp.int32, (values.shape[0], 128), 1)
        st[rows, :] = jnp.where(lanes == stat_lane, scale, st[rows, :])

    def qkv(first, count):
        rows = pl.ds(first, count)
        a = a1[rows, :]
        for part, ref in enumerate((q, k, v)):
            for j in range(3):
                cols = slice(j * 256, j * 256 + 256)
                m = dot(a, wqkv[:, part * D + j * 256 : part * D + j * 256 + 256])
                if part == 0:
                    m = (m + query_bias[:, cols]) * 0.125
                if part == 2:
                    m = m + value_bias[:, cols]
                ref[rows, cols] = m.astype(bf16)

    st[...] = jnp.zeros_like(st)

    def one_side(which):
        first = pl.multiple_of(which * SLOT, 16)
        limit = jnp.where(which == 0, images, captions)
        keep = lax.broadcasted_iota(jnp.int32, (SLOT, 1), 0) < limit
        bias = jnp.where(which == 0, proj_b[0:1, :].astype(f32), proj_b[1:2, :].astype(f32))
        for j in range(3):
            cols = slice(j * 256, j * 256 + 256)
            p = (dot(raw[which], pw[which, :, cols]) + bias[:, cols]).astype(bf16)
            x[pl.ds(first, SLOT), cols] = jnp.where(keep, p, 0).astype(bf16)

        def norm_step(i):
            rows = pl.ds(pl.multiple_of(first + i * 112, 16), 112)
            normed(x[rows, :].astype(f32), rows, gain1, shift1, xh1, a1, 12)

        for i in range(3):
            norm_step(i)
        qkv(first, SLOT)

    x[CLS:NR, :] = jnp.where(
        lax.broadcasted_iota(jnp.int32, (NR - CLS, 1), 0) == 0, row_of(cls), 0.0
    ).astype(bf16)
    normed(x[CLS:NR, :].astype(f32), slice(CLS, NR), gain1, shift1, xh1, a1, 12)
    load("wqkv")
    qkv(CLS, NR - CLS)
    one_side(side)
    exchange.wait()
    one_side(1 - side)
    put(raw, raw_o)
    put(xh1, xh1_o)
    put(a1, a1_o)
    put(q, q_o)
    put(k, k_o)
    put(v, v_o)

    def attend(i):
        p, block = divmod(i, NR // QUERY_ROWS)
        rows, cols = slice(block * QUERY_ROWS, (block + 1) * QUERY_ROWS), slice(p * 128, p * 128 + 128)
        queries, keys, values = q[rows, cols], k[:, cols], v[:, cols]
        both, kept_stats = [], st[rows, :]
        for head in range(2):
            s = dot(jnp.where(lane // 64 == head, queries, 0).astype(bf16), keys, NT) + key_bias
            peak = jnp.max(s, axis=-1, keepdims=True)
            e = jnp.exp(s - peak)
            total = jnp.sum(e, axis=-1, keepdims=True)
            both.append(dot(e.astype(bf16), values) * (1.0 / total))
            kept_stats = jnp.where(lane == 2 * p + head, peak + jnp.log(total), kept_stats)
        o[rows, cols] = jnp.where(lane < 64, both[0], both[1]).astype(bf16)
        st[rows, :] = kept_stats

    for i in range(6 * (NR // QUERY_ROWS)):
        attend(i)
    put(o, o_o)
    load("wo")
    out_bias = row_of(out_b)
    for j in range(3):
        cols = slice(j * 256, j * 256 + 256)
        h[:, cols] = x[:, cols].astype(f32) + dot(o[...], wo[:, cols]) + out_bias[:, cols]
    gain2, shift2 = row_of(mlp_gain), row_of(mlp_shift)

    def norm_two(i):
        rows = slice(i * 176, i * 176 + 176)
        normed(h[rows, :], rows, gain2, shift2, xh2, a2, 13)

    for i in range(NR // 176):
        norm_two(i)
    put(st, st_o)
    put(h, h_o)
    put(xh2, xh2_o)
    put(a2, a2_o)
    load("wup")
    up_bias = row_of(up_b)
    for j in range(12):
        cols = slice(j * 256, j * 256 + 256)
        u = dot(a2[...], wup[:, cols]) + up_bias[:, cols]
        value, slope = gelu_both(u)
        g[:, cols] = value.astype(bf16)
        gp[:, cols] = slope.astype(bf16)
    put(g, g_o)
    put(gp, gp_o)
    for copy in stores:
        copy.wait()


BLOCK = 384
D_, U_, A_, B_, P_ = range(5)
BLOCKS = (4, 4, 2, 2, 2)
SLOTS = (0, 0, 0, 2, 0)
STAGES = 9


class Comm:
    def __init__(self, refs, outs):
        self.gs, self.go, self.ssem, self.rsem, self.lsem, self.tiny, self.tbuf, self.tsem = refs[:8]
        n = len(BLOCKS)
        self.hx, self.ra, self.rb, self.r2, self.r3 = (refs[8 + n * j : 8 + n * j + n] for j in range(5))
        self.outs = outs
        self.xyz, self.core = coords()

    def greet(self):
        signal(device(self.xyz, 1 - self.core))
        for axis in range(3):
            for by in (1, 2, 3):
                signal(device(along(self.xyz, axis, by), self.core))
        pl.semaphore_wait(pltpu.get_barrier_semaphore(), 10)

    def sizes(self, i):
        rows = BLOCKS[i] * BLOCK
        return rows, rows // 4, rows // 8, rows // 16

    def send(self, i, sem, src, dst, place, core=None):
        target = device(place, self.core if core is None else core)
        remote(src, dst, self.ssem.at[i, sem], self.rsem.at[i, sem], target).start()

    def wait(self, i, sem, ref, sent=False):
        copy = remote(ref, ref, self.ssem.at[i, sem], self.rsem.at[i, sem], device(self.xyz, 1 - self.core))
        if sent:
            copy.wait_send()
        else:
            copy.wait_recv()

    def amount(self, i, stage):
        return {1: self.ra, 2: self.rb, 3: self.r2, 4: self.r2, 5: self.r2, 6: self.ra, 7: self.rb, 8: self.hx}[
            stage
        ][i]

    def emit(self, i, b, tile):
        slot = SLOTS[i] + b
        self.gs[slot] = tile(pl.multiple_of((1 - self.core) * BLOCK, BLOCK)).astype(bf16)
        dst = self.hx[i].at[b * BLOCK : (b + 1) * BLOCK]
        self.send(i, STAGES + b, self.gs.at[slot], dst, self.xyz, 1 - self.core)
        self.go[slot] = tile(pl.multiple_of(self.core * BLOCK, BLOCK)).astype(bf16)

    def start(self, i, stage):
        hx, xyz = self.hx[i], self.xyz
        _, q1, half, q2 = self.sizes(i)
        if stage == 8:
            for b in range(BLOCKS[i]):
                src = hx.at[b * BLOCK : (b + 1) * BLOCK]
                dst = self.outs[i].at[pl.ds(b * D + self.core * BLOCK, BLOCK)]
                self.send(i, 8, src, dst, xyz, 1 - self.core)
                pltpu.make_async_copy(src, dst, self.lsem.at[i]).start()
            return
        for k in range(3):
            cols = pl.ds(k * 256, 256)
            axis = (k + {1: 0, 2: 0, 3: 1, 4: 2, 5: 1, 6: 0, 7: 0}[stage]) % 3
            at = [along(xyz, axis, by) for by in range(4)]
            right, across, left = at[1], at[2], at[3]

            def part(place, second=0, size=half):
                return hx.at[pl.ds(place[axis] * q1 + second * half, size), cols]

            if stage == 1:
                ra = self.ra[i]
                self.send(i, 1, part(across, 0), ra.at[k, 2], left)
                self.send(i, 1, part(across, 1), ra.at[k, 3], right)
                self.send(i, 1, part(left, 1), ra.at[k, 1], left)
                self.send(i, 1, part(right, 0), ra.at[k, 0], right)
            if stage == 2:
                self.send(i, 2, part(left, 0), self.rb[i].at[k, 0], left)
                self.send(i, 2, part(right, 1), self.rb[i].at[k, 1], right)
            if stage == 6:
                for place in (left, right):
                    mine = part(xyz, 0, q1)
                    self.send(i, 6, mine, mine, place)
            if stage == 7:
                for place, src in ((right, part(left, 0)), (left, part(right, 1))):
                    self.send(i, 7, src, src, place)
            for by in (2, 1, 3):
                if stage == 3:
                    src = hx.at[pl.ds(xyz[k] * q1 + at[by][axis] * q2, q2), cols]
                    self.send(i, 3, src, self.r2[i].at[k, by - 1], at[by])
                if stage == 4:
                    src = self.r3[i].at[k, xyz[axis]]
                    self.send(i, 4, src, src, at[by])
                if stage == 5:
                    src = hx.at[pl.ds(xyz[k] * q1 + xyz[axis] * q2, q2), cols]
                    self.send(i, 5, src, src, at[by])

    def add_in(self, i, first, k, size, terms):
        step = min(size, 96)
        hx = self.hx[i]

        def body(j):
            rows = pl.ds(pl.multiple_of(first + j * step, 16), step)
            v = hx[rows, pl.ds(k * 256, 256)].astype(f32)
            for ref, at in terms:
                v = v + ref[k, at, span(j, step), :].astype(f32)
            hx[rows, pl.ds(k * 256, 256)] = v.astype(bf16)

        loop(size // step, body)

    def take(self, i, stage):
        hx, xyz = self.hx[i], self.xyz
        _, q1, half, q2 = self.sizes(i)
        if stage == 0:
            for b in range(BLOCKS[i]):
                rows = slice(b * BLOCK, (b + 1) * BLOCK)
                self.wait(i, STAGES + b, self.gs.at[b])
                self.wait(i, STAGES + b, self.gs.at[b], sent=True)

                def body(j):
                    r = span(j, 96)
                    at = span(j, 96, b * BLOCK)
                    hx[at, :] = (self.go[SLOTS[i] + b, r, :].astype(f32) + hx[at, :].astype(f32)).astype(bf16)

                loop(BLOCK // 96, body)
            return
        self.wait(i, stage, self.amount(i, stage))
        self.wait(i, stage, self.amount(i, stage), sent=True)
        for k in range(3):
            own = xyz[k] * q1
            if stage == 1:
                left, right = along(xyz, k, 3)[k], along(xyz, k, 1)[k]
                self.add_in(i, left * q1, k, half, [(self.ra[i], 2)])
                self.add_in(i, right * q1 + half, k, half, [(self.ra[i], 3)])
            if stage == 2:
                self.add_in(i, own, k, half, [(self.ra[i], 0), (self.rb[i], 0)])
                self.add_in(i, own + half, k, half, [(self.ra[i], 1), (self.rb[i], 1)])
            if stage == 3:
                first = pl.multiple_of(own + xyz[(k + 1) % 3] * q2, 16)
                v = hx[pl.ds(first, q2), pl.ds(k * 256, 256)].astype(f32)
                for d in range(3):
                    v = v + self.r2[i][k, d].astype(f32)
                self.r3[i][k, xyz[(k + 2) % 3]] = v.astype(bf16)
            if stage == 4:
                v = self.r3[i][k, 0].astype(f32)
                for d in range(1, 4):
                    v = v + self.r3[i][k, d].astype(f32)
                first = pl.multiple_of(own + xyz[(k + 1) % 3] * q2, 16)
                hx[pl.ds(first, q2), pl.ds(k * 256, 256)] = v.astype(bf16)

    def advance(self, i, stage):
        self.take(i, stage - 1)
        self.start(i, stage)

    def finish(self):
        for i in range(len(BLOCKS)):
            self.wait(i, 8, self.hx[i])
            pltpu.make_async_copy(self.hx[i], self.hx[i], self.lsem.at[i]).wait()
            self.wait(i, 8, self.hx[i], sent=True)


    def tiny_copies(self, step):
        core, xyz = self.core, self.xyz
        part = self.tbuf.at[step, core if step == 0 else xyz[step - 1]]
        pairs = [(device(xyz, 1 - core), 0)]
        if step > 0:
            pairs = [(device(along(xyz, step - 1, by), core), by - 1) for by in (2, 1, 3)]
        return [
            remote(part, part, self.tsem.at[0, step, j], self.tsem.at[1, step, j], target)
            for target, j in pairs
        ]

    def tiny_stage(self, step):
        if step == 0:
            self.tbuf[0, self.core] = self.tiny[...]
        else:
            for copy in self.tiny_copies(step - 1):
                copy.wait()
            v = self.tbuf[step - 1, 0]
            for d in range(1, 2 if step == 1 else 4):
                v = v + self.tbuf[step - 1, d]
            if step < 4:
                self.tbuf[step, self.xyz[step - 1]] = v
            else:
                self.tiny[...] = v
        if step < 4:
            for copy in self.tiny_copies(step):
                copy.start()


COMM_SCRATCH = [
    pltpu.VMEM((4, BLOCK, D), bf16),
    pltpu.VMEM((4, BLOCK, D), bf16),
    pltpu.SemaphoreType.DMA((len(BLOCKS), STAGES + 4)),
    pltpu.SemaphoreType.DMA((len(BLOCKS), STAGES + 4)),
    pltpu.SemaphoreType.DMA((len(BLOCKS),)),
    pltpu.VMEM((16, D), f32),
    pltpu.VMEM((4, 4, 16, D), f32),
    pltpu.SemaphoreType.DMA((2, 4, 3)),
    *[pltpu.VMEM((n * BLOCK, D), bf16) for n in BLOCKS],
    *[pltpu.VMEM((3, 4, n * BLOCK // 8, 256), bf16) for n in BLOCKS],
    *[pltpu.VMEM((3, 2, n * BLOCK // 8, 256), bf16) for n in BLOCKS],
    *[pltpu.VMEM((3, 3, n * BLOCK // 16, 256), bf16) for n in BLOCKS],
    *[pltpu.VMEM((3, 4, n * BLOCK // 16, 256), bf16) for n in BLOCKS],
]

SCHEDULE = {
    "dUa": [(D_, 1)],
    "dA2": [(U_, 1), (D_, 2)],
    "att0": [(U_, 2)],
    "att1a": [(D_, 3)],
    "att2a": [(U_, 3)],
    "att3a": [(D_, 4)],
    "att4a": [(U_, 4)],
    "att5a": [(D_, 5)],
    "A": [(U_, 5)],
    "B": [(A_, 1), (D_, 6)],
    "dA1": [(B_, 1), (U_, 6)],
    "N1": [(A_, 2)],
    "P": ["t0"],
    "back": [(D_, 7), "t1"],
    "out0": [(P_, 1), (B_, 2)],
    "out1": ["t2"],
    "out2": [(U_, 7)],
    "end": [(A_, 3), (D_, 8), "t3", (P_, 2), (B_, 3), "t4", (U_, 8), (A_, 4), (P_, 3), (B_, 4),
        (A_, 5), (P_, 4), (B_, 5), (A_, 6), (P_, 5), (B_, 6), (A_, 7), (P_, 6), (B_, 7), (A_, 8),
        (P_, 7), (B_, 8), (P_, 8)],
}

KEY_ROWS = 352
WO = 3 * D
WP = 4 * D


def backward_kernel(
    assignment, image_class, caption_length,
    cotangent, raw_i, xh1_i, a1_i, q_i, k_i, v_i, st_i, o_i, h_i, xh2_i, a2_i, g_i, gp_i,
    proj_w, qkv_w, out_w, up_w, down_w, attn_gain, mlp_gain, down_b,
    layer_out, o0, o1, o2, o3, o4, tiny_o, back_o,
    W, GA, GB, dy, a2, xh2, a1, xh1, raw, stc, stt, da, dh, dp, acc, dq_s, kt, sg, lsem, bsem, *comm_scratch,
):
    comm = Comm(comm_scratch, (o0, o1, o2, o3, o4))
    xyz, core, tiny, emit = comm.xyz, comm.core, comm.tiny, comm.emit
    partner = device(along(xyz, 0, 2), core)
    side, _, images, captions = item_sizes(assignment, image_class, caption_length, xyz, core)

    def hook(name):
        for due in SCHEDULE.get(name, ()):
            if isinstance(due, str):
                comm.tiny_stage(int(due[1]))
            else:
                comm.advance(*due)

    def columns(ref, count, size=D):
        return [ref.at[:, b * size : b * size + size] for b in range(count)]

    load = Loads(lsem)
    load.start("g", *zip(columns(g_i, 4), [GA.at[b] for b in range(4)]))
    load.start("wd", (down_w, W.at[0:FF]))
    load.start("gp", *zip(columns(gp_i, 4), [GB.at[b] for b in range(4)]))
    load.start("a2", (a2_i, a2))
    load.start("wu", *zip(columns(up_w, 4), [W.at[FF + b * D : FF + b * D + D] for b in range(4)]))
    load.start("st", (st_i, stc))
    load.start("xh2", (xh2_i, xh2))
    comm.greet()

    row = lax.broadcasted_iota(jnp.int32, (NR, 1), 0)
    valid_col = valid_of(row, images, captions)
    key_bias = jnp.where(valid_col, 0.0, MASKED)
    thirds = [slice(j * 256, j * 256 + 256) for j in range(3)]
    for cols in thirds:
        da[0:SEQ, cols] = cotangent[0, 0, :, cols].astype(f32)
        v = da[:, cols]
        v = jnp.where(row == CLS, v[0:1, :], pltpu.roll(v, NR - 1, 0))
        dy[:, cols] = jnp.where(valid_col, v, 0.0).astype(bf16)

    ones = jnp.ones((16, NR), bf16)

    def column_sums(at, value):
        tiny[at : at + 1, :] = dot(ones[:, : value.shape[0]], value)[0:1, :]

    def weight_grad(i, b, left, right):
        emit(i, b, lambda first: dot(left[:, pl.ds(first, BLOCK)], right[...], TN))

    load("g")
    for b in range(4):
        weight_grad(D_, b, GA.at[b], dy)
    hook("D")
    load.start("qkvo", (q_i, GA.at[0]), (k_i, GA.at[1]), (v_i, GA.at[2]), (o_i, GA.at[3]))
    load.start("a1", (a1_i, a1))
    load.start("xh1", (xh1_i, xh1))
    load.start("raw", (raw_i, raw))
    column_sums(14, dy[...])
    load("wd")
    load("gp")

    def gate_grad(b):
        for cols in thirds:
            v = dot(dy[...], W[b * D + cols.start : b * D + cols.stop, :], NT)
            GB[b, :, cols] = (v * GB[b, :, cols].astype(f32)).astype(bf16)

    gate_grad(0)
    gate_grad(1)
    hook("dUa")
    gate_grad(2)
    gate_grad(3)
    hook("dUb")
    load.start("wqkv", *zip(columns(qkv_w, 3), [W.at[b * D : b * D + D] for b in range(3)]))
    load.start("wo", (out_w, W.at[WO : WO + D]))
    load("a2")
    for b in range(4):
        weight_grad(U_, b, a2, GB.at[b])
        column_sums(10 + b, GB[b])
    hook("U")

    def input_grad(first, blocks):
        for cols in thirds:
            v = dot(GB[0], W[first + cols.start : first + cols.stop, :], NT)
            for b in range(1, blocks):
                v = v + dot(GB[b], W[first + b * D + cols.start : first + b * D + cols.stop, :], NT)
            da[:, cols] = v

    load("wu")
    input_grad(FF, 4)
    load.start("pw", (proj_w.at[0], W.at[WP : WP + D]), (proj_w.at[1], W.at[WP + D : WP + 2 * D]))
    hook("dA2")

    def norm_back(gain_ref, xh_ref, stat_lane, add_to, at):
        gain = row_of(gain_ref)
        acc[...] = jnp.zeros_like(acc)
        for i in range(NR // NORM_ROWS):
            rows = slice(i * NORM_ROWS, (i + 1) * NORM_ROWS)
            d, xh, scale = da[rows, :], xh_ref[rows, :].astype(f32), stc[rows, stat_lane : stat_lane + 1]
            gg = d * gain
            m1 = jnp.mean(gg, axis=-1, keepdims=True)
            m2 = jnp.mean(gg * xh, axis=-1, keepdims=True)
            dh[rows, :] = add_to(rows) + scale * (gg - m1 - xh * m2)
            acc[0] += jnp.sum((d * xh).reshape(NORM_ROWS // 8, 8, D), axis=0)
            acc[1] += jnp.sum(d.reshape(NORM_ROWS // 8, 8, D), axis=0)
        tiny[at : at + 1, :] = jnp.sum(acc[0], axis=0, keepdims=True)
        tiny[at + 1 : at + 2, :] = jnp.sum(acc[1], axis=0, keepdims=True)

    load("xh2")
    load("st")
    norm_back(mlp_gain, xh2, 13, lambda rows: dy[rows, :].astype(f32), 8)
    dy[...] = dh[...].astype(bf16)
    hook("N2")
    load("qkvo")
    queries, keys, values, attended = (GA.at[b] for b in range(4))
    d_q, d_k, d_v, d_o = (GB.at[b] for b in range(4))
    load("wo")
    for cols in thirds:
        d_o[:, cols] = dot(dy[...], W[WO + cols.start : WO + cols.stop, :], NT).astype(bf16)
    weight_grad(A_, 0, attended, dy)
    column_sums(7, dy[...])
    hook("dO")
    stt[...] = jnp.transpose(stc[...])
    lane = lax.broadcasted_iota(jnp.int32, (NR, 128), 1)
    head_of = lax.broadcasted_iota(jnp.int32, (16, 128), 1) // 64
    select = (head_of == lax.broadcasted_iota(jnp.int32, (16, 128), 0)).astype(bf16)

    for p in range(6):
        cols = slice(p * 128, p * 128 + 128)
        qq, kk, vv, do = queries[:, cols], keys[:, cols], values[:, cols], d_o[:, cols]
        product = do.astype(f32) * attended[:, cols].astype(f32)
        high = product.astype(bf16)
        low = (product - high.astype(f32)).astype(bf16)
        delta = dot(select, high, NT) + dot(select, low, NT)
        kt[...] = jnp.transpose(kk)
        dk = dv = 0.0
        for head in range(2):
            q_of = jnp.where(lane // 64 == head, qq, 0).astype(bf16)
            do_of = jnp.where(lane // 64 == head, do, 0).astype(bf16)
            s = dot(kk, q_of, NT) + key_bias - stt[2 * p + head : 2 * p + head + 1, :]
            pr = jnp.exp(s)
            dpr = dot(vv, do_of, NT)
            ds = (pr * (dpr - delta[head : head + 1, :])).astype(bf16)
            dv = dv + dot(pr.astype(bf16), do_of)
            dk = dk + dot(ds, q_of)
            dq_s[head * 64 : head * 64 + 64, :] = dot(kt[head * 64 : head * 64 + 64, :], ds)
            if head == 0:
                hook("att%da" % p)
        d_k[:, cols] = dk.astype(bf16)
        d_v[:, cols] = dv.astype(bf16)
        d_q[:, cols] = (jnp.transpose(dq_s[...]).astype(bf16).astype(f32) * 0.125).astype(bf16)
        hook("att%d" % p)
    load.start("g2", *zip(columns(g_i, 4), [GA.at[b] for b in range(4)]))
    load("a1")
    weight_grad(A_, 1, a1, d_q)
    hook("A")
    weight_grad(B_, 0, a1, d_k)
    weight_grad(B_, 1, a1, d_v)
    hook("B")
    column_sums(5, d_q[...])
    column_sums(6, d_v[...])
    load("wqkv")
    input_grad(0, 3)
    load.start("wd2", (down_w, W.at[0:FF]))
    hook("dA1")
    load("xh1")
    norm_back(attn_gain, xh1, 12, lambda rows: dh[rows, :], 3)
    load.start("h", (h_i, da))
    tiny[0:1, :] = dh[CLS : CLS + 1, :]
    tiny[15:16, :] = jnp.zeros((1, D), f32)
    hook("N1")
    load("raw")
    for s in range(2):
        dp[s] = dh[s * SLOT : (s + 1) * SLOT, :].astype(bf16)
    for s in range(2):
        weight_grad(P_, s, raw.at[s], dp.at[s])
        column_sums(1 + s, dp[s])
    hook("P")
    load("pw")

    def states_back(which, slot):
        for j in range(3):
            v = dot(dp[which], W[span(j, 256, WP + which * D), :], NT)
            sg[slot, :, j * 256 : j * 256 + 256] = v.astype(bf16)

    states_back(1 - side, 1)
    returned = remote(sg.at[1], back_o.at[1], bsem.at[0], bsem.at[1], partner)
    returned.start()
    states_back(side, 0)
    own = pltpu.make_async_copy(sg.at[0], back_o.at[0], bsem.at[2])
    own.start()
    hook("back")
    load("g2")
    load("wd2")
    load("h")
    down_bias = row_of(down_b)
    valid = valid_col.astype(f32)
    for cols in thirds:
        y = da[:, cols] + down_bias[:, cols]
        for b in range(4):
            y = y + dot(GA[b], W[b * D : b * D + D, cols])
        y = y * valid
        y = jnp.where(row == 0, y[CLS : CLS + 1, :], pltpu.roll(y, 1, 0))
        layer_out[0, 0, :, cols] = y[:SEQ].astype(bf16)
        hook("out%d" % (cols.start // 256))
    hook("end")
    final = pltpu.make_async_copy(tiny, tiny_o, bsem.at[3])
    final.start()
    comm.finish()
    final.wait()
    own.wait()
    returned.wait()


PIECE = 768


def unpack_kernel(
    assignment, back, c0, c1, c2, c3, c4, tiny_i,
    states_grad, cls, proj_w, proj_b, attn_gain, attn_shift, qkv_w, query_b, value_b, out_w, out_b,
    mlp_gain, mlp_shift, up_w, up_b, down_w, down_b,
    src, dst, tiny, pair, isem, osem, bsem,
):
    xyz, core = coords()
    side = xyz[0] // 2
    group = ((lax.rem(xyz[0], 2) * 2 + xyz[2] // 2) * 4 + xyz[1]) * 2 + core
    chosen = assignment[0, group]
    kept = jnp.where(side == 0, chosen, 1 - chosen)
    moves = [
        pltpu.make_async_copy(back, pair, bsem.at[0]),
        pltpu.make_async_copy(pair.at[0], states_grad.at[0, 0, kept], bsem.at[1]),
        pltpu.make_async_copy(pair.at[1], states_grad.at[0, 0, 1 - kept], bsem.at[2]),
        pltpu.make_async_copy(tiny_i, tiny, bsem.at[3]),
    ]
    moves[0].start()
    moves[3].start()
    blocks = []
    for b in range(4):
        blocks.append((c0, b, down_w.at[b * D : b * D + D]))
    for b in range(4):
        blocks.append((c1, b, up_w.at[:, b * D : b * D + D]))
    blocks.append((c2, 0, out_w))
    for b, (chunk, at) in enumerate(((c2, 1), (c3, 0), (c3, 1))):
        blocks.append((chunk, at, qkv_w.at[:, b * D : b * D + D]))
    for b in range(2):
        blocks.append((c4, b, proj_w.at[b]))
    n = len(blocks)
    depth = 4

    def read(i):
        chunk, at, _ = blocks[i]
        return pltpu.make_async_copy(chunk.at[at * D : at * D + D], src.at[i % depth], isem.at[i % depth])

    def write(i):
        return pltpu.make_async_copy(dst.at[i % depth], blocks[i][2], osem.at[i % depth])

    for i in range(depth):
        read(i).start()
    for i in range(n):
        if i == 2:
            moves[0].wait()
            moves[1].start()
            moves[2].start()
        read(i).wait()
        if i >= depth:
            write(i - depth).wait()

        def body(j):
            dst[i % depth, span(j, 64), :] = src[i % depth, span(j, 64), :].astype(f32)

        loop(D // 64, body)
        write(i).start()
        if i + depth < n:
            read(i + depth).start()
    moves[3].wait()
    for ref, at in ((cls, 0), (attn_gain, 3), (attn_shift, 4), (query_b, 5), (value_b, 6), (out_b, 7), (mlp_gain, 8), (mlp_shift, 9), (down_b, 14)):
        ref[...] = tiny[at : at + 1, :].reshape(D)
    proj_b[...] = tiny[1:3, :]
    for b in range(4):
        up_b[pl.ds(b * D, D)] = tiny[10 + b : 11 + b, :].reshape(D)
    for i in range(n - depth, n):
        write(i).wait()
    moves[1].wait()
    moves[2].wait()


def shape(*dims, dtype=bf16):
    return jax.ShapeDtypeStruct(dims, dtype)


def scratch(*dims, dtype=bf16):
    return pltpu.VMEM(dims, dtype)


ANY = pl.BlockSpec(memory_space=pl.ANY)
VMEM = pl.BlockSpec(memory_space=pltpu.VMEM)
SMEM = pl.BlockSpec(memory_space=pltpu.SMEM)
DMA = pltpu.SemaphoreType.DMA
ITEM = (NR, D)


def per_device(
    side_states, assignment, image_class, caption_length, cls_token, proj_weight, proj_bias,
    attn_gain, attn_shift, qkv_weight, query_bias, value_bias, out_weight, out_bias,
    mlp_gain, mlp_shift, up_weight, up_bias, down_weight, down_bias, out_cotangent,
):
    sizes = (assignment, jnp.swapaxes(image_class, 1, 2), jnp.swapaxes(caption_length, 1, 2))
    raw, xh1, a1, q, k, v, st, o, h, xh2, a2, g, gp = pl.pallas_call(
        forward_kernel,
        out_shape=[
            shape(2, SLOT, D), shape(*ITEM), shape(*ITEM), shape(*ITEM), shape(*ITEM), shape(*ITEM),
            shape(NR, 128, dtype=f32), shape(*ITEM), shape(*ITEM, dtype=f32), shape(*ITEM), shape(*ITEM),
            shape(NR, FF), shape(NR, FF),
        ],
        in_specs=[SMEM] * 3 + [ANY] * 5 + [VMEM] * 10,
        out_specs=[ANY] * 13,
        scratch_shapes=[
            scratch(2, SLOT, D), scratch(SLOT, D), scratch(2, SLOT, D),
            scratch(2, D, D), scratch(D, 3 * D), scratch(D, D), scratch(D, FF),
            scratch(*ITEM), scratch(*ITEM), scratch(*ITEM), scratch(*ITEM), scratch(*ITEM), scratch(*ITEM),
            scratch(NR, 128, dtype=f32), scratch(*ITEM), scratch(*ITEM, dtype=f32), scratch(*ITEM), scratch(*ITEM),
            scratch(NR, FF), scratch(NR, FF), DMA((5,)), DMA((13,)), DMA((2,)),
        ],
        compiler_params=pltpu.CompilerParams(collective_id=0, has_side_effects=True, vmem_limit_bytes=62 * MIB),
        name="forward",
    )(
        *sizes, side_states, proj_weight, qkv_weight, out_weight, up_weight,
        cls_token, proj_bias, attn_gain, attn_shift, query_bias, value_bias, out_bias,
        mlp_gain, mlp_shift, up_bias,
    )
    layer_out, *chunks, tiny, back = pl.pallas_call(
        backward_kernel,
        out_shape=[shape(1, 1, SEQ, D)]
        + [shape(n * D, D) for n in BLOCKS]
        + [shape(16, D, dtype=f32), shape(2, SLOT, D)],
        in_specs=[SMEM] * 3 + [VMEM] + [ANY] * 18 + [VMEM] * 3,
        out_specs=[VMEM] + [ANY] * (len(BLOCKS) + 2),
        scratch_shapes=[
            scratch(8 * D, D), scratch(4, *ITEM), scratch(4, *ITEM),
            scratch(*ITEM), scratch(*ITEM), scratch(*ITEM), scratch(*ITEM), scratch(*ITEM), scratch(2, SLOT, D),
            scratch(NR, 128, dtype=f32), scratch(128, NR, dtype=f32),
            scratch(*ITEM, dtype=f32), scratch(*ITEM, dtype=f32), scratch(2, SLOT, D),
            scratch(2, 8, D, dtype=f32), scratch(128, NR, dtype=f32), scratch(128, NR), scratch(2, SLOT, D),
            DMA((40,)), DMA((4,)), *COMM_SCRATCH,
        ],
        compiler_params=pltpu.CompilerParams(collective_id=1, has_side_effects=True, vmem_limit_bytes=63 * MIB),
        name="backward",
    )(
        *sizes, out_cotangent, raw, xh1, a1, q, k, v, st, o, h, xh2, a2, g, gp,
        proj_weight, qkv_weight, out_weight, up_weight, down_weight, attn_gain, mlp_gain, down_bias,
    )
    vector = shape(D, dtype=f32)
    grads = pl.pallas_call(
        unpack_kernel,
        out_shape=[
            shape(1, 1, 2, SLOT, D), vector, shape(2, D, D, dtype=f32), shape(2, D, dtype=f32), vector, vector,
            shape(D, 3 * D, dtype=f32), vector, vector, shape(D, D, dtype=f32), vector, vector, vector,
            shape(D, FF, dtype=f32), shape(FF, dtype=f32), shape(FF, D, dtype=f32), vector,
        ],
        in_specs=[SMEM] + [ANY] * (len(BLOCKS) + 2),
        out_specs=[ANY, VMEM, ANY, VMEM, VMEM, VMEM, ANY, VMEM, VMEM, ANY, VMEM, VMEM, VMEM, ANY, VMEM, ANY, VMEM],
        scratch_shapes=[
            scratch(4, PIECE, D), scratch(4, PIECE, D, dtype=f32), scratch(16, D, dtype=f32), scratch(2, SLOT, D),
            DMA((4,)), DMA((4,)), DMA((4,)),
        ],
        compiler_params=pltpu.CompilerParams(vmem_limit_bytes=62 * MIB),
        name="unpack",
    )(assignment, back, *chunks, tiny)
    return (layer_out, *grads)


def solution(mesh):
    weights = (P(),) * 16
    return jax.shard_map(
        per_device,
        mesh=mesh,
        in_specs=(P("items", "tower"), P("items"), P("items"), P("items"), *weights, P("items", "tower")),
        out_specs=(P("items", "tower"), P("items", "tower"), *weights),
        check_vma=False,
    )
```

```python
import jax
import jax.numpy as jnp
from jax import lax
from jax.experimental import pallas as pl
from jax.experimental.pallas import tpu as pltpu
from jax.sharding import PartitionSpec as P

bf16 = jnp.bfloat16
f32 = jnp.float32
MESH = pl.DeviceIdType.MESH
D = 768
FF = 3072
SLOT = 336
SEQ = 673
SMALL_PATCHES = 197
LARGE_PATCHES = 325
NR = 704
CLS = 2 * SLOT
EPS = 1e-5
MASKED = -1e30
MIB = 2**20

NN = (((1,), (0,)), ((), ()))
NT = (((1,), (1,)), ((), ()))
TN = (((0,), (0,)), ((), ()))


def dot(a, b, dims=NN):
    return lax.dot_general(a, b, dims, preferred_element_type=f32)


def loop(n, body, start=0):
    def step(i, carry):
        body(i)
        return carry

    lax.fori_loop(start, n, step, 0)


def span(i, n, base=0):
    return pl.ds(pl.multiple_of(base + i * n, n), n)


def row_of(ref):
    return ref[...].astype(f32).reshape(1, ref.shape[0])


def coords():
    items, tower = lax.axis_index("items"), lax.axis_index("tower")
    x, y = tower // 16, lax.rem(tower // 2, 4)
    return (x, y, lax.rem(tower // 8, 2) * 2 + items), lax.rem(tower, 2)


def device(xyz, core):
    x, y, z = xyz
    return lax.rem(z, 2), ((x * 2 + z // 2) * 4 + y) * 2 + core


def along(xyz, axis, by):
    place = list(xyz)
    place[axis] = lax.rem(place[axis] + by, 4)
    return tuple(place)


def signal(target):
    pl.semaphore_signal(
        pltpu.get_barrier_semaphore(), inc=1, device_id=target, device_id_type=MESH
    )


def remote(src, dst, send, recv, target):
    return pltpu.make_async_remote_copy(
        src_ref=src,
        dst_ref=dst,
        send_sem=send,
        recv_sem=recv,
        device_id=target,
        device_id_type=MESH,
    )


def item_sizes(assignment, image_class, caption_length, xyz, core):
    side = xyz[0] // 2
    group = ((lax.rem(xyz[0], 2) * 2 + xyz[2] // 2) * 4 + xyz[1]) * 2 + core
    chosen = assignment[0, group]
    kept = jnp.where(side == 0, chosen, 1 - chosen)
    images = jnp.where(image_class[0, kept, group] == 1, LARGE_PATCHES, SMALL_PATCHES)
    return side, kept, images, caption_length[0, kept, group]


def valid_of(index, images, captions):
    ok = (index < images) | ((index >= SLOT) & (index < SLOT + captions)) | (index == CLS)
    return ok


class Loads:
    def __init__(self, sem):
        self.sem, self.copies, self.count = sem, {}, 0

    def start(self, name, *pairs):
        self.copies[name] = []
        for src, dst in pairs:
            copy = pltpu.make_async_copy(src, dst, self.sem.at[self.count])
            self.count += 1
            copy.start()
            self.copies[name].append(copy)

    def __call__(self, name):
        for copy in self.copies[name]:
            copy.wait()


def stats(v):
    mean = jnp.mean(v, axis=-1, keepdims=True)
    center = v - mean
    var = jnp.mean(center * center, axis=-1, keepdims=True)
    return center, lax.rsqrt(var + EPS)


GELU_A = 0.7978845608028654
GELU_B = 0.044715


def gelu_both(u):
    u2 = u * u
    t = jnp.tanh(u * (GELU_A + (GELU_A * GELU_B) * u2))
    half = 0.5 + 0.5 * t
    slope = half + (0.5 * u) * (1.0 - t * t) * (GELU_A + (3 * GELU_A * GELU_B) * u2)
    return u * half, slope


NORM_ROWS = 176
QUERY_ROWS = 352
KEY_ROWS = 352


BLOCK = 384
D_, U_, A_, B_, P_ = range(5)
BLOCKS = (4, 4, 2, 2, 2)
SLOTS = (0, 0, 0, 2, 0)
STAGES = 9


class Comm:
    def __init__(self, refs, outs):
        self.gs, self.go, self.ssem, self.rsem, self.lsem, self.tiny, self.tbuf, self.tsem = refs[:8]
        n = len(BLOCKS)
        self.hx = refs[8 : 8 + n]
        self.ra, self.rb, self.r2, self.r3 = (self.slots(*refs[8 + n + 2 * j : 10 + n + 2 * j]) for j in range(4))
        self.outs = outs
        self.xyz, self.core = coords()

    def slots(self, first, second):
        half = first.shape[2] // 2
        low, high = first.at[:, :, 0:half], first.at[:, :, half : 2 * half]
        return first, second, low, high, second.at[:, :, 0:half]

    def greet(self):
        signal(device(self.xyz, 1 - self.core))
        for axis in range(3):
            for by in (1, 2, 3):
                signal(device(along(self.xyz, axis, by), self.core))
        pl.semaphore_wait(pltpu.get_barrier_semaphore(), 10)

    def sizes(self, i):
        rows = BLOCKS[i] * BLOCK
        return rows, rows // 4, rows // 8, rows // 16

    def send(self, i, sem, src, dst, place, core=None):
        target = device(place, self.core if core is None else core)
        remote(src, dst, self.ssem.at[i, sem], self.rsem.at[i, sem], target).start()

    def wait(self, i, sem, ref, sent=False):
        copy = remote(ref, ref, self.ssem.at[i, sem], self.rsem.at[i, sem], device(self.xyz, 1 - self.core))
        if sent:
            copy.wait_send()
        else:
            copy.wait_recv()

    def amount(self, i, stage):
        return {1: self.ra, 2: self.rb, 3: self.r2, 4: self.r2, 5: self.r2, 6: self.ra, 7: self.rb, 8: self.hx}[
            stage
        ][i]

    def emit(self, i, b, tile):
        slot = SLOTS[i] + b
        self.gs[slot] = tile(pl.multiple_of((1 - self.core) * BLOCK, BLOCK)).astype(bf16)
        dst = self.hx[i].at[b * BLOCK : (b + 1) * BLOCK]
        self.send(i, STAGES + b, self.gs.at[slot], dst, self.xyz, 1 - self.core)
        self.go[slot] = tile(pl.multiple_of(self.core * BLOCK, BLOCK)).astype(bf16)

    def start(self, i, stage):
        hx, xyz = self.hx[i], self.xyz
        _, q1, half, q2 = self.sizes(i)
        if stage == 8:
            for b in range(BLOCKS[i]):
                src = hx.at[b * BLOCK : (b + 1) * BLOCK]
                dst = self.outs[i].at[pl.ds(b * D + self.core * BLOCK, BLOCK)]
                self.send(i, 8, src, dst, xyz, 1 - self.core)
                pltpu.make_async_copy(src, dst, self.lsem.at[i]).start()
            return
        for k in range(3):
            cols = pl.ds(k * 256, 256)
            axis = (k + {1: 0, 2: 0, 3: 1, 4: 2, 5: 1, 6: 0, 7: 0}[stage]) % 3
            at = [along(xyz, axis, by) for by in range(4)]
            right, across, left = at[1], at[2], at[3]

            def part(place, second=0, size=half):
                return hx.at[pl.ds(place[axis] * q1 + second * half, size), cols]

            if stage == 1:
                ra = self.ra[i]
                self.send(i, 1, part(across, 0), ra.at[k, 2], left)
                self.send(i, 1, part(across, 1), ra.at[k, 3], right)
                self.send(i, 1, part(left, 1), ra.at[k, 1], left)
                self.send(i, 1, part(right, 0), ra.at[k, 0], right)
            if stage == 2:
                self.send(i, 2, part(left, 0), self.rb[i].at[k, 0], left)
                self.send(i, 2, part(right, 1), self.rb[i].at[k, 1], right)
            if stage == 6:
                for place in (left, right):
                    mine = part(xyz, 0, q1)
                    self.send(i, 6, mine, mine, place)
            if stage == 7:
                for place, src in ((right, part(left, 0)), (left, part(right, 1))):
                    self.send(i, 7, src, src, place)
            for by in (2, 1, 3):
                if stage == 3:
                    src = hx.at[pl.ds(xyz[k] * q1 + at[by][axis] * q2, q2), cols]
                    self.send(i, 3, src, self.r2[i].at[k, by - 1], at[by])
                if stage == 4:
                    src = self.r3[i].at[k, xyz[axis]]
                    self.send(i, 4, src, src, at[by])
                if stage == 5:
                    src = hx.at[pl.ds(xyz[k] * q1 + xyz[axis] * q2, q2), cols]
                    self.send(i, 5, src, src, at[by])

    def add_in(self, i, first, k, size, terms):
        step = min(size, 96)
        hx = self.hx[i]

        def body(j):
            rows = pl.ds(pl.multiple_of(first + j * step, 16), step)
            v = hx[rows, pl.ds(k * 256, 256)].astype(f32)
            for ref, at in terms:
                v = v + ref[k, at, span(j, step), :].astype(f32)
            hx[rows, pl.ds(k * 256, 256)] = v.astype(bf16)

        loop(size // step, body)

    def take(self, i, stage):
        hx, xyz = self.hx[i], self.xyz
        _, q1, half, q2 = self.sizes(i)
        if stage == 0:
            for b in range(BLOCKS[i]):
                rows = slice(b * BLOCK, (b + 1) * BLOCK)
                self.wait(i, STAGES + b, self.gs.at[b])
                self.wait(i, STAGES + b, self.gs.at[b], sent=True)

                def body(j):
                    r = span(j, 96)
                    at = span(j, 96, b * BLOCK)
                    hx[at, :] = (self.go[SLOTS[i] + b, r, :].astype(f32) + hx[at, :].astype(f32)).astype(bf16)

                loop(BLOCK // 96, body)
            return
        self.wait(i, stage, self.amount(i, stage))
        self.wait(i, stage, self.amount(i, stage), sent=True)
        for k in range(3):
            own = xyz[k] * q1
            if stage == 1:
                left, right = along(xyz, k, 3)[k], along(xyz, k, 1)[k]
                self.add_in(i, left * q1, k, half, [(self.ra[i], 2)])
                self.add_in(i, right * q1 + half, k, half, [(self.ra[i], 3)])
            if stage == 2:
                self.add_in(i, own, k, half, [(self.ra[i], 0), (self.rb[i], 0)])
                self.add_in(i, own + half, k, half, [(self.ra[i], 1), (self.rb[i], 1)])
            if stage == 3:
                first = pl.multiple_of(own + xyz[(k + 1) % 3] * q2, 16)
                v = hx[pl.ds(first, q2), pl.ds(k * 256, 256)].astype(f32)
                for d in range(3):
                    v = v + self.r2[i][k, d].astype(f32)
                self.r3[i][k, xyz[(k + 2) % 3]] = v.astype(bf16)
            if stage == 4:
                v = self.r3[i][k, 0].astype(f32)
                for d in range(1, 4):
                    v = v + self.r3[i][k, d].astype(f32)
                first = pl.multiple_of(own + xyz[(k + 1) % 3] * q2, 16)
                hx[pl.ds(first, q2), pl.ds(k * 256, 256)] = v.astype(bf16)

    def advance(self, i, stage):
        self.take(i, stage - 1)
        self.start(i, stage)

    def finish(self):
        for i in range(len(BLOCKS)):
            self.wait(i, 8, self.hx[i])
            pltpu.make_async_copy(self.hx[i], self.hx[i], self.lsem.at[i]).wait()
            self.wait(i, 8, self.hx[i], sent=True)


    def tiny_copies(self, step):
        core, xyz = self.core, self.xyz
        part = self.tbuf.at[step, core if step == 0 else xyz[step - 1]]
        pairs = [(device(xyz, 1 - core), 0)]
        if step > 0:
            pairs = [(device(along(xyz, step - 1, by), core), by - 1) for by in (2, 1, 3)]
        return [
            remote(part, part, self.tsem.at[0, step, j], self.tsem.at[1, step, j], target)
            for target, j in pairs
        ]

    def tiny_stage(self, step):
        if step == 0:
            self.tbuf[0, self.core] = self.tiny[...]
        else:
            for copy in self.tiny_copies(step - 1):
                copy.wait()
            v = self.tbuf[step - 1, 0]
            for d in range(1, 2 if step == 1 else 4):
                v = v + self.tbuf[step - 1, d]
            if step < 4:
                self.tbuf[step, self.xyz[step - 1]] = v
            else:
                self.tiny[...] = v
        if step < 4:
            for copy in self.tiny_copies(step):
                copy.start()


COMM_SCRATCH = [
    pltpu.VMEM((4, BLOCK, D), bf16),
    pltpu.VMEM((4, BLOCK, D), bf16),
    pltpu.SemaphoreType.DMA((len(BLOCKS), STAGES + 4)),
    pltpu.SemaphoreType.DMA((len(BLOCKS), STAGES + 4)),
    pltpu.SemaphoreType.DMA((len(BLOCKS),)),
    pltpu.VMEM((16, D), f32),
    pltpu.VMEM((4, 4, 16, D), f32),
    pltpu.SemaphoreType.DMA((2, 4, 3)),
    *[pltpu.VMEM((n * BLOCK, D), bf16) for n in BLOCKS],
    *[pltpu.VMEM((3, 4, n * BLOCK // 8, 256), bf16) for n in BLOCKS[:2]],
    *[pltpu.VMEM((3, 2, n * BLOCK // 8, 256), bf16) for n in BLOCKS[:2]],
    *[pltpu.VMEM((3, 3, n * BLOCK // 16, 256), bf16) for n in BLOCKS[:2]],
    *[pltpu.VMEM((3, 4, n * BLOCK // 16, 256), bf16) for n in BLOCKS[:2]],
]

SCHEDULE = {
    "dUa": [(D_, 1)],
    "dA2": [(U_, 1), (D_, 2)],
    "att0": [(U_, 2)],
    "att1a": [(D_, 3)],
    "att2a": [(U_, 3)],
    "att3a": [(D_, 4)],
    "att4a": [(U_, 4)],
    "att5a": [(D_, 5)],
    "A": [(U_, 5)],
    "B": [(A_, 1), (D_, 6)],
    "dA1": [(B_, 1), (U_, 6)],
    "N1": [(A_, 2)],
    "P": ["t0"],
    "back": [(P_, 1), (D_, 7), "t1"],
    "out0": [(B_, 2)],
    "out1": ["t2"],
    "out2": [(U_, 7)],
    "end": [(A_, 3), (D_, 8), "t3", (P_, 2), (B_, 3), "t4", (U_, 8), (A_, 4), (P_, 3), (B_, 4),
        (A_, 5), (P_, 4), (B_, 5), (A_, 6), (P_, 5), (B_, 6), (A_, 7), (P_, 6), (B_, 7), (A_, 8),
        (P_, 7), (B_, 8), (P_, 8)],
}

WO = 3 * D
WP = 4 * D


def layer_kernel(
    assignment, image_class, caption_length,
    cotangent, states, proj_w, qkv_w, out_w, up_w, down_w,
    cls, proj_b, attn_gain, attn_shift, query_b, value_b, out_b, mlp_gain, mlp_shift, up_b, down_b,
    layer_out, o0, o1, o2, o3, o4, tiny_o, back_o, xh1_o, h_o,
    W, GA, GB, GC, dy, xh, a1, a2, raw, stc, stt, da, dh, acc, dq_s, kt, lsem, bsem, *comm_scratch,
):
    comm = Comm(comm_scratch, (o0, o1, o2, o3, o4))
    xyz, core, tiny, emit = comm.xyz, comm.core, comm.tiny, comm.emit
    partner = device(along(xyz, 0, 2), core)
    side, kept, images, captions = item_sizes(assignment, image_class, caption_length, xyz, core)

    def hook(name):
        for due in SCHEDULE.get(name, ()):
            if isinstance(due, str):
                comm.tiny_stage(int(due[1]))
            else:
                comm.advance(*due)

    def hook_at(step, names):
        for at in range(6):
            if SCHEDULE.get(names % at):

                @pl.when(step == at)
                def _():
                    hook(names % at)

    def columns(ref, count, first=0):
        return [ref.at[:, b * D : b * D + D] for b in range(first, first + count)]

    def weight_rows(first, count):
        return [W.at[first + b * D : first + b * D + D] for b in range(count)]

    def load_attention():
        load.start("wqkv", *zip(columns(qkv_w, 3), weight_rows(0, 3)))
        load.start("wo", (out_w, W.at[WO : WO + D]))

    def load_proj():
        load.start("pw", *zip([proj_w.at[0], proj_w.at[1]], weight_rows(WP, 2)))

    load = Loads(lsem)
    x, h, sent = a2, da, comm.gs.at[0, 0:SLOT]
    sg, dp = [[GC.at[b, 0:SLOT] for b in pair] for pair in ((0, 1), (2, 3))]
    load.start("states", *[(states.at[0, 0, b], sg[b]) for b in range(2)])
    load_proj()
    load_attention()
    load.start("wu2", *zip(columns(up_w, 2, 2), weight_rows(FF + 2 * D, 2)))
    comm.greet()
    load("states")
    sent[...] = jnp.where(kept == 0, sg[1][...], sg[0][...])
    pieces = ((0, 176), (176, 160))
    exchange = [
        remote(sent.at[a : a + n], raw.at[side, a : a + n], bsem.at[4, j], bsem.at[5, j], partner)
        for j, (a, n) in enumerate(pieces)
    ]
    for copy in exchange:
        copy.start()
    raw[side] = jnp.where(kept == 0, sg[0][...], sg[1][...])

    def valid_rows():
        row = lax.broadcasted_iota(jnp.int32, (NR, 1), 0)
        return row, valid_of(row, images, captions)

    key_row = lax.broadcasted_iota(jnp.int32, (1, NR), 1)
    key_bias_row = jnp.where(valid_of(key_row, images, captions), 0.0, MASKED)
    thirds = [slice(j * 256, j * 256 + 256) for j in range(3)]
    gain1, shift1 = row_of(attn_gain), row_of(attn_shift)
    query_bias, value_bias = row_of(query_b), row_of(value_b)
    half_lane = lax.broadcasted_iota(jnp.int32, (QUERY_ROWS, 128), 1)

    def normed(values, rows, gain, shift, a_ref, stat_lane):
        center, scale = stats(values)
        unit = center * scale
        xh[rows, :] = unit.astype(bf16)
        a_ref[rows, :] = (unit * gain + shift).astype(bf16)
        lanes = lax.broadcasted_iota(jnp.int32, (values.shape[0], 128), 1)
        stc[rows, :] = jnp.where(lanes == stat_lane, scale, stc[rows, :])

    def qkv(rows):
        a = a1[rows, :]
        for part in range(3):
            for cols in thirds:
                m = dot(a, W[part * D : part * D + D, cols])
                if part == 0:
                    m = (m + query_bias[:, cols]) * 0.125
                if part == 2:
                    m = m + value_bias[:, cols]
                GC[part, rows, cols] = m.astype(bf16)

    stc[...] = jnp.zeros_like(stc)

    def one_side(which, start, count):
        rows = pl.ds(pl.multiple_of(which * SLOT + start, 16), count)
        limit = jnp.where(which == 0, images, captions)
        keep = lax.broadcasted_iota(jnp.int32, (count, 1), 0) + start < limit
        bias = jnp.where(which == 0, proj_b[0:1, :].astype(f32), proj_b[1:2, :].astype(f32))
        inputs = raw[which, start : start + count, :]
        first = pl.multiple_of(WP + which * D, 16)
        for cols in thirds:
            p = (dot(inputs, W[pl.ds(first, D), cols]) + bias[:, cols]).astype(bf16)
            x[rows, cols] = jnp.where(keep, p, 0).astype(bf16)
        normed(x[rows, :].astype(f32), rows, gain1, shift1, a1, 12)
        qkv(rows)

    x[CLS:NR, :] = jnp.where(
        lax.broadcasted_iota(jnp.int32, (NR - CLS, 1), 0) == 0, row_of(cls), 0.0
    ).astype(bf16)
    normed(x[CLS:NR, :].astype(f32), slice(CLS, NR), gain1, shift1, a1, 12)
    load("pw")
    load("wqkv")
    qkv(slice(CLS, NR))
    one_side(side, 0, 176)
    one_side(side, 176, 160)
    row, valid_col = valid_rows()
    for cols in thirds:
        dh[0:SEQ, cols] = cotangent[0, 0, :, cols].astype(f32)
        v = dh[:, cols]
        v = jnp.where(row == CLS, v[0:1, :], pltpu.roll(v, NR - 1, 0))
        dy[:, cols] = jnp.where(valid_col, v, 0.0).astype(bf16)
    for copy, (a, n) in zip(exchange, pieces):
        copy.wait()
        one_side(1 - side, a, n)
    load.start("wu0", *zip(columns(up_w, 2), weight_rows(FF, 2)))
    load.start("xh1 out", (xh, xh1_o))

    queries, keys, values, attended = (GC.at[b] for b in range(4))

    def attend(p, block):
        rows, cols = slice(block * QUERY_ROWS, (block + 1) * QUERY_ROWS), span(p, 128)
        qq, kk, vv = queries[rows, cols], keys[:, cols], values[:, cols]
        both, kept_stats = [], stc[rows, :]
        for head in range(2):
            q_of = jnp.where(half_lane // 64 == head, qq, 0).astype(bf16)
            s = dot(q_of, kk, NT) + key_bias_row
            peak = jnp.max(s, axis=-1, keepdims=True)
            e = jnp.exp(s - peak)
            total = jnp.sum(e, axis=-1, keepdims=True)
            both.append(dot(e.astype(bf16), vv) * (1.0 / total))
            kept_stats = jnp.where(half_lane == 2 * p + head, peak + jnp.log(total), kept_stats)
        attended[rows, cols] = jnp.where(half_lane < 64, both[0], both[1]).astype(bf16)
        stc[rows, :] = kept_stats

    def attend_pairs(i):
        for p in range(1):
            for block in range(NR // QUERY_ROWS):
                attend(i * 1 + p, block)

    loop(6, attend_pairs)
    load("wo")
    out_bias = row_of(out_b)
    for cols in thirds:
        h[:, cols] = x[:, cols].astype(f32) + dot(attended[...], W[WO : WO + D, cols]) + out_bias[:, cols]
    load.start("wd", (down_w, W.at[0:FF]))
    load.start("h out", (h, h_o))
    load("xh1 out")
    gain2, shift2 = row_of(mlp_gain), row_of(mlp_shift)
    for i in range(NR // NORM_ROWS):
        rows = slice(i * NORM_ROWS, (i + 1) * NORM_ROWS)
        normed(h[rows, :], rows, gain2, shift2, a2, 13)
    load("wu2")
    load("wu0")
    up_bias = row_of(up_b)
    for b in range(4):
        for cols in thirds:
            u = dot(a2[...], W[FF + b * D : FF + b * D + D, cols])
            u = u + up_bias[:, b * D + cols.start : b * D + cols.stop]
            value, slope = gelu_both(u)
            GA[b, :, cols] = value.astype(bf16)
            GB[b, :, cols] = slope.astype(bf16)

    ones = jnp.ones((16, NR), bf16)

    def column_sums(at, value):
        tiny[at : at + 1, :] = dot(ones[:, : value.shape[0]], value)[0:1, :]

    def weight_grad(i, b, left, right):
        emit(i, b, lambda first: dot(left[:, pl.ds(first, BLOCK)], right[...], TN))

    for b in range(4):
        weight_grad(D_, b, GA.at[b], dy)
    hook("D")
    column_sums(14, dy[...])
    load("wd")
    load("h out")

    def gate_grad(b):
        for cols in thirds:
            v = dot(dy[...], W[b * D + cols.start : b * D + cols.stop, :], NT)
            GB[b, :, cols] = (v * GB[b, :, cols].astype(f32)).astype(bf16)

    gate_grad(0)
    gate_grad(1)
    hook("dUa")
    gate_grad(2)
    gate_grad(3)
    hook("dUb")
    load_attention()
    for b in range(4):
        weight_grad(U_, b, a2, GB.at[b])
        column_sums(10 + b, GB[b])
    hook("U")

    def input_grad(first, blocks):
        for cols in thirds:
            v = dot(GB[0], W[first + cols.start : first + cols.stop, :], NT)
            for b in range(1, blocks):
                v = v + dot(GB[b], W[first + b * D + cols.start : first + b * D + cols.stop, :], NT)
            da[:, cols] = v

    input_grad(FF, 4)
    load_proj()
    hook("dA2")

    def norm_back(gain_ref, xh_ref, stat_lane, add_to, at):
        gain = row_of(gain_ref)
        acc[...] = jnp.zeros_like(acc)
        for i in range(NR // NORM_ROWS):
            rows = slice(i * NORM_ROWS, (i + 1) * NORM_ROWS)
            d, xh, scale = da[rows, :], xh_ref[rows, :].astype(f32), stc[rows, stat_lane : stat_lane + 1]
            gg = d * gain
            m1 = jnp.mean(gg, axis=-1, keepdims=True)
            m2 = jnp.mean(gg * xh, axis=-1, keepdims=True)
            dh[rows, :] = add_to(rows) + scale * (gg - m1 - xh * m2)
            acc[0] += jnp.sum((d * xh).reshape(NORM_ROWS // 8, 8, D), axis=0)
            acc[1] += jnp.sum(d.reshape(NORM_ROWS // 8, 8, D), axis=0)
        tiny[at : at + 1, :] = jnp.sum(acc[0], axis=0, keepdims=True)
        tiny[at + 1 : at + 2, :] = jnp.sum(acc[1], axis=0, keepdims=True)

    norm_back(mlp_gain, xh, 13, lambda rows: dy[rows, :].astype(f32), 8)
    dy[...] = dh[...].astype(bf16)
    load.start("xh1", (xh1_o, xh))
    hook("N2")
    d_q, d_k, d_v, d_o = (GB.at[b] for b in range(4))
    load("wo")
    for cols in thirds:
        d_o[:, cols] = dot(dy[...], W[WO + cols.start : WO + cols.stop, :], NT).astype(bf16)
    weight_grad(A_, 0, attended, dy)
    column_sums(7, dy[...])
    hook("dO")
    stt[...] = jnp.transpose(stc[...])
    key_bias = jnp.where(valid_rows()[1], 0.0, MASKED)
    lane = lax.broadcasted_iota(jnp.int32, (NR, 128), 1)
    head_of = lax.broadcasted_iota(jnp.int32, (16, 128), 1) // 64
    select = (head_of == lax.broadcasted_iota(jnp.int32, (16, 128), 0)).astype(bf16)

    def attend_back(p):
        cols = span(p, 128)
        qq, do = queries[:, cols], d_o[:, cols]
        product = do.astype(f32) * attended[:, cols].astype(f32)
        high = product.astype(bf16)
        low = (product - high.astype(f32)).astype(bf16)
        delta = dot(select, high, NT) + dot(select, low, NT)
        for kb in range(NR // KEY_ROWS):
            kt[kb] = jnp.transpose(keys[kb * KEY_ROWS : (kb + 1) * KEY_ROWS, cols])
        q_of = [jnp.where(lane // 64 == head, qq, 0).astype(bf16) for head in range(2)]
        do_of = [jnp.where(lane // 64 == head, do, 0).astype(bf16) for head in range(2)]
        dq = [0.0, 0.0]
        for kb in range(NR // KEY_ROWS):
            rows = slice(kb * KEY_ROWS, (kb + 1) * KEY_ROWS)
            kk, vv = keys[rows, cols], values[rows, cols]
            dk = dv = 0.0
            for head in range(2):
                s = dot(kk, q_of[head], NT) + key_bias[rows] - stt[pl.ds(2 * p + head, 1), :]
                pr = jnp.exp(s)
                dpr = dot(vv, do_of[head], NT)
                ds = (pr * (dpr - delta[head : head + 1, :])).astype(bf16)
                dv = dv + dot(pr.astype(bf16), do_of[head])
                dk = dk + dot(ds, q_of[head])
                dq[head] = dq[head] + dot(kt[kb, head * 64 : head * 64 + 64, :], ds)
            d_k[rows, cols] = dk.astype(bf16)
            d_v[rows, cols] = dv.astype(bf16)
            if kb == 0:
                hook_at(p, "att%da")
        for head in range(2):
            dq_s[head * 64 : head * 64 + 64, :] = dq[head]
        d_q[:, cols] = (jnp.transpose(dq_s[...]).astype(bf16).astype(f32) * 0.125).astype(bf16)
        hook_at(p, "att%d")

    loop(6, attend_back)
    weight_grad(A_, 1, a1, d_q)
    hook("A")
    weight_grad(B_, 0, a1, d_k)
    weight_grad(B_, 1, a1, d_v)
    hook("B")
    column_sums(5, d_q[...])
    column_sums(6, d_v[...])
    load("wqkv")
    input_grad(0, 3)
    load.start("wd2", (down_w, W.at[0:FF]))
    hook("dA1")
    load("xh1")
    norm_back(attn_gain, xh, 12, lambda rows: dh[rows, :], 3)
    load.start("h", (h_o, da))
    tiny[0:1, :] = dh[CLS : CLS + 1, :]
    tiny[15:16, :] = jnp.zeros((1, D), f32)
    hook("N1")
    for s in range(2):
        dp[s][...] = dh[s * SLOT : (s + 1) * SLOT, :].astype(bf16)
    for s in range(2):
        weight_grad(P_, s, raw.at[s], dp[s])
        column_sums(1 + s, dp[s][...])
    hook("P")
    load("pw")

    def states_back(which, slot):
        for j in range(3):
            v = dot(GC[2 + which, 0:SLOT, :], W[span(j, 256, WP + which * D), :], NT)
            sg[slot][:, j * 256 : j * 256 + 256] = v.astype(bf16)

    states_back(1 - side, 1)
    returned = remote(sg[1], back_o.at[1], bsem.at[0, 0], bsem.at[1, 0], partner)
    returned.start()
    states_back(side, 0)
    own = pltpu.make_async_copy(sg[0], back_o.at[0], bsem.at[2, 0])
    own.start()
    hook("back")
    load("wd2")
    load("h")
    down_bias = row_of(down_b)
    row, valid_col = valid_rows()
    valid = valid_col.astype(f32)
    for cols in thirds:
        y = da[:, cols] + down_bias[:, cols]
        for b in range(4):
            y = y + dot(GA[b], W[b * D : b * D + D, cols])
        y = y * valid
        y = jnp.where(row == 0, y[CLS : CLS + 1, :], pltpu.roll(y, 1, 0))
        layer_out[0, 0, :, cols] = y[:SEQ].astype(bf16)
        hook("out%d" % (cols.start // 256))
    hook("end")
    final = pltpu.make_async_copy(tiny, tiny_o, bsem.at[3, 0])
    final.start()
    comm.finish()
    final.wait()
    own.wait()
    returned.wait()


PIECE = 768


def unpack_kernel(
    assignment, back, c0, c1, c2, c3, c4, tiny_i,
    states_grad, cls, proj_w, proj_b, attn_gain, attn_shift, qkv_w, query_b, value_b, out_w, out_b,
    mlp_gain, mlp_shift, up_w, up_b, down_w, down_b,
    src, dst, tiny, pair, isem, osem, bsem,
):
    xyz, core = coords()
    side = xyz[0] // 2
    group = ((lax.rem(xyz[0], 2) * 2 + xyz[2] // 2) * 4 + xyz[1]) * 2 + core
    chosen = assignment[0, group]
    kept = jnp.where(side == 0, chosen, 1 - chosen)
    moves = [
        pltpu.make_async_copy(back, pair, bsem.at[0]),
        pltpu.make_async_copy(pair.at[0], states_grad.at[0, 0, kept], bsem.at[1]),
        pltpu.make_async_copy(pair.at[1], states_grad.at[0, 0, 1 - kept], bsem.at[2]),
        pltpu.make_async_copy(tiny_i, tiny, bsem.at[3]),
    ]
    moves[0].start()
    moves[3].start()
    blocks = []
    for b in range(4):
        blocks.append((c0, b, down_w.at[b * D : b * D + D]))
    for b in range(4):
        blocks.append((c1, b, up_w.at[:, b * D : b * D + D]))
    blocks.append((c2, 0, out_w))
    for b, (chunk, at) in enumerate(((c2, 1), (c3, 0), (c3, 1))):
        blocks.append((chunk, at, qkv_w.at[:, b * D : b * D + D]))
    for b in range(2):
        blocks.append((c4, b, proj_w.at[b]))
    n = len(blocks)
    depth = 4

    def read(i):
        chunk, at, _ = blocks[i]
        return pltpu.make_async_copy(chunk.at[at * D : at * D + D], src.at[i % depth], isem.at[i % depth])

    def write(i):
        return pltpu.make_async_copy(dst.at[i % depth], blocks[i][2], osem.at[i % depth])

    for i in range(depth):
        read(i).start()
    for i in range(n):
        if i == 2:
            moves[0].wait()
            moves[1].start()
            moves[2].start()
        read(i).wait()
        if i >= depth:
            write(i - depth).wait()

        def body(j):
            dst[i % depth, span(j, 64), :] = src[i % depth, span(j, 64), :].astype(f32)

        loop(D // 64, body)
        write(i).start()
        if i + depth < n:
            read(i + depth).start()
    moves[3].wait()
    for ref, at in ((cls, 0), (attn_gain, 3), (attn_shift, 4), (query_b, 5), (value_b, 6), (out_b, 7), (mlp_gain, 8), (mlp_shift, 9), (down_b, 14)):
        ref[...] = tiny[at : at + 1, :].reshape(D)
    proj_b[...] = tiny[1:3, :]
    for b in range(4):
        up_b[pl.ds(b * D, D)] = tiny[10 + b : 11 + b, :].reshape(D)
    for i in range(n - depth, n):
        write(i).wait()
    moves[1].wait()
    moves[2].wait()


def shape(*dims, dtype=bf16):
    return jax.ShapeDtypeStruct(dims, dtype)


def scratch(*dims, dtype=bf16):
    return pltpu.VMEM(dims, dtype)


ANY = pl.BlockSpec(memory_space=pl.ANY)
VMEM = pl.BlockSpec(memory_space=pltpu.VMEM)
SMEM = pl.BlockSpec(memory_space=pltpu.SMEM)
DMA = pltpu.SemaphoreType.DMA
ITEM = (NR, D)


def per_device(
    side_states, assignment, image_class, caption_length, cls_token, proj_weight, proj_bias,
    attn_gain, attn_shift, qkv_weight, query_bias, value_bias, out_weight, out_bias,
    mlp_gain, mlp_shift, up_weight, up_bias, down_weight, down_bias, out_cotangent,
):
    sizes = (assignment, jnp.swapaxes(image_class, 1, 2), jnp.swapaxes(caption_length, 1, 2))
    layer_out, *chunks, tiny, back, _, _ = pl.pallas_call(
        layer_kernel,
        out_shape=[shape(1, 1, SEQ, D)]
        + [shape(n * D, D) for n in BLOCKS]
        + [shape(16, D, dtype=f32), shape(2, SLOT, D), shape(*ITEM), shape(*ITEM, dtype=f32)],
        in_specs=[SMEM] * 3 + [VMEM] + [ANY] * 6 + [VMEM] * 11,
        out_specs=[VMEM] + [ANY] * (len(BLOCKS) + 4),
        scratch_shapes=[
            scratch(8 * D, D), scratch(4, *ITEM), scratch(4, *ITEM), scratch(4, *ITEM),
            scratch(*ITEM), scratch(*ITEM), scratch(*ITEM), scratch(*ITEM), scratch(2, SLOT, D),
            scratch(NR, 128, dtype=f32), scratch(128, NR, dtype=f32),
            scratch(*ITEM, dtype=f32), scratch(*ITEM, dtype=f32),
            scratch(2, 8, D, dtype=f32), scratch(128, NR, dtype=f32), scratch(2, 128, KEY_ROWS),
            DMA((40,)), DMA((6, 2)), *COMM_SCRATCH,
        ],
        compiler_params=pltpu.CompilerParams(
            collective_id=0, has_side_effects=True, vmem_limit_bytes=63 * MIB
        ),
        name="layer",
    )(
        *sizes, out_cotangent, side_states, proj_weight, qkv_weight, out_weight, up_weight, down_weight,
        cls_token, proj_bias, attn_gain, attn_shift, query_bias, value_bias, out_bias,
        mlp_gain, mlp_shift, up_bias, down_bias,
    )
    vector = shape(D, dtype=f32)
    grads = pl.pallas_call(
        unpack_kernel,
        out_shape=[
            shape(1, 1, 2, SLOT, D), vector, shape(2, D, D, dtype=f32), shape(2, D, dtype=f32), vector, vector,
            shape(D, 3 * D, dtype=f32), vector, vector, shape(D, D, dtype=f32), vector, vector, vector,
            shape(D, FF, dtype=f32), shape(FF, dtype=f32), shape(FF, D, dtype=f32), vector,
        ],
        in_specs=[SMEM] + [ANY] * (len(BLOCKS) + 2),
        out_specs=[ANY, VMEM, ANY, VMEM, VMEM, VMEM, ANY, VMEM, VMEM, ANY, VMEM, VMEM, VMEM, ANY, VMEM, ANY, VMEM],
        scratch_shapes=[
            scratch(4, PIECE, D), scratch(4, PIECE, D, dtype=f32), scratch(16, D, dtype=f32), scratch(2, SLOT, D),
            DMA((4,)), DMA((4,)), DMA((4,)),
        ],
        compiler_params=pltpu.CompilerParams(vmem_limit_bytes=62 * MIB),
        name="unpack",
    )(assignment, back, *chunks, tiny)
    return (layer_out, *grads)


def solution(mesh):
    weights = (P(),) * 16
    return jax.shard_map(
        per_device,
        mesh=mesh,
        in_specs=(P("items", "tower"), P("items"), P("items"), P("items"), *weights, P("items", "tower")),
        out_specs=(P("items", "tower"), P("items", "tower"), *weights),
        check_vma=False,
    )
```

```python
import jax
import jax.numpy as jnp
from jax import lax
from jax.experimental import pallas as pl
from jax.experimental.pallas import tpu as pltpu
from jax.sharding import PartitionSpec as P

bf16 = jnp.bfloat16
f32 = jnp.float32
MESH = pl.DeviceIdType.MESH
D = 768
FF = 3072
SLOT = 336
SEQ = 673
SMALL_PATCHES = 197
LARGE_PATCHES = 325
NR = 704
CLS = 2 * SLOT
EPS = 1e-5
MASKED = -1e30
MIB = 2**20

NN = (((1,), (0,)), ((), ()))
NT = (((1,), (1,)), ((), ()))
TN = (((0,), (0,)), ((), ()))


def dot(a, b, dims=NN):
    return lax.dot_general(a, b, dims, preferred_element_type=f32)


def loop(n, body, start=0):
    def step(i, carry):
        body(i)
        return carry

    lax.fori_loop(start, n, step, 0)


def span(i, n, base=0):
    return pl.ds(pl.multiple_of(base + i * n, n), n)


def row_of(ref):
    return ref[...].astype(f32).reshape(1, ref.shape[0])


def coords():
    items, tower = lax.axis_index("items"), lax.axis_index("tower")
    x, y = tower // 16, lax.rem(tower // 2, 4)
    return (x, y, lax.rem(tower // 8, 2) * 2 + items), lax.rem(tower, 2)


def device(xyz, core):
    x, y, z = xyz
    return lax.rem(z, 2), ((x * 2 + z // 2) * 4 + y) * 2 + core


def along(xyz, axis, by):
    place = list(xyz)
    place[axis] = lax.rem(place[axis] + by, 4)
    return tuple(place)


def signal(target):
    pl.semaphore_signal(
        pltpu.get_barrier_semaphore(), inc=1, device_id=target, device_id_type=MESH
    )


def remote(src, dst, send, recv, target):
    return pltpu.make_async_remote_copy(
        src_ref=src,
        dst_ref=dst,
        send_sem=send,
        recv_sem=recv,
        device_id=target,
        device_id_type=MESH,
    )


def item_sizes(assignment, image_class, caption_length, xyz, core):
    side = xyz[0] // 2
    group = ((lax.rem(xyz[0], 2) * 2 + xyz[2] // 2) * 4 + xyz[1]) * 2 + core
    chosen = assignment[0, group]
    kept = jnp.where(side == 0, chosen, 1 - chosen)
    images = jnp.where(image_class[0, kept, group] == 1, LARGE_PATCHES, SMALL_PATCHES)
    return side, kept, images, caption_length[0, kept, group]


def valid_of(index, images, captions):
    ok = (index < images) | ((index >= SLOT) & (index < SLOT + captions)) | (index == CLS)
    return ok


class Loads:
    def __init__(self, sem):
        self.sem, self.copies, self.count = sem, {}, 0

    def start(self, name, *pairs):
        self.copies[name] = []
        for src, dst in pairs:
            copy = pltpu.make_async_copy(src, dst, self.sem.at[self.count])
            self.count += 1
            copy.start()
            self.copies[name].append(copy)

    def __call__(self, name):
        for copy in self.copies[name]:
            copy.wait()


def stats(v):
    mean = jnp.mean(v, axis=-1, keepdims=True)
    center = v - mean
    var = jnp.mean(center * center, axis=-1, keepdims=True)
    return center, lax.rsqrt(var + EPS)


GELU_A = 0.7978845608028654
GELU_B = 0.044715


def gelu_both(u):
    u2 = u * u
    t = jnp.tanh(u * (GELU_A + (GELU_A * GELU_B) * u2))
    half = 0.5 + 0.5 * t
    slope = half + (0.5 * u) * (1.0 - t * t) * (GELU_A + (3 * GELU_A * GELU_B) * u2)
    return u * half, slope


NORM_ROWS = 176
QUERY_ROWS = 352
KEY_ROWS = 352


BLOCK = 384
D_, U_, A_, B_, P_ = range(5)
BLOCKS = (4, 4, 2, 2, 2)
SLOTS = (0, 0, 0, 2, 0)
STAGES = 9


class Comm:
    def __init__(self, refs, outs):
        self.gs, self.go, self.ssem, self.rsem, self.lsem, self.tiny, self.tbuf, self.tsem = refs[:8]
        n = len(BLOCKS)
        self.hx = refs[8 : 8 + n]
        self.ra, self.rb, self.r2, self.r3 = (self.slots(*refs[8 + n + 2 * j : 10 + n + 2 * j]) for j in range(4))
        self.outs = outs
        self.xyz, self.core = coords()

    def slots(self, first, second):
        half = first.shape[2] // 2
        low, high = first.at[:, :, 0:half], first.at[:, :, half : 2 * half]
        return first, second, low, high, second.at[:, :, 0:half]

    def greet(self):
        signal(device(self.xyz, 1 - self.core))
        for axis in range(3):
            for by in (1, 2, 3):
                signal(device(along(self.xyz, axis, by), self.core))
        pl.semaphore_wait(pltpu.get_barrier_semaphore(), 10)

    def sizes(self, i):
        rows = BLOCKS[i] * BLOCK
        return rows, rows // 4, rows // 8, rows // 16

    def send(self, i, sem, src, dst, place, core=None):
        target = device(place, self.core if core is None else core)
        remote(src, dst, self.ssem.at[i, sem], self.rsem.at[i, sem], target).start()

    def wait(self, i, sem, ref, sent=False):
        copy = remote(ref, ref, self.ssem.at[i, sem], self.rsem.at[i, sem], device(self.xyz, 1 - self.core))
        if sent:
            copy.wait_send()
        else:
            copy.wait_recv()

    def amount(self, i, stage):
        return {1: self.ra, 2: self.rb, 3: self.r2, 4: self.r2, 5: self.r2, 6: self.ra, 7: self.rb, 8: self.hx}[
            stage
        ][i]

    def emit(self, i, b, tile):
        slot = SLOTS[i] + b
        self.gs[slot] = tile(pl.multiple_of((1 - self.core) * BLOCK, BLOCK)).astype(bf16)
        dst = self.hx[i].at[b * BLOCK : (b + 1) * BLOCK]
        self.send(i, STAGES + b, self.gs.at[slot], dst, self.xyz, 1 - self.core)
        self.go[slot] = tile(pl.multiple_of(self.core * BLOCK, BLOCK)).astype(bf16)

    def start(self, i, stage):
        hx, xyz = self.hx[i], self.xyz
        _, q1, half, q2 = self.sizes(i)
        if stage == 8:
            for b in range(BLOCKS[i]):
                src = hx.at[b * BLOCK : (b + 1) * BLOCK]
                dst = self.outs[i].at[pl.ds(b * D + self.core * BLOCK, BLOCK)]
                self.send(i, 8, src, dst, xyz, 1 - self.core)
                pltpu.make_async_copy(src, dst, self.lsem.at[i]).start()
            return
        for k in range(3):
            cols = pl.ds(k * 256, 256)
            axis = (k + {1: 0, 2: 0, 3: 1, 4: 2, 5: 1, 6: 0, 7: 0}[stage]) % 3
            at = [along(xyz, axis, by) for by in range(4)]
            right, across, left = at[1], at[2], at[3]

            def part(place, second=0, size=half):
                return hx.at[pl.ds(place[axis] * q1 + second * half, size), cols]

            if stage == 1:
                ra = self.ra[i]
                self.send(i, 1, part(across, 0), ra.at[k, 2], left)
                self.send(i, 1, part(across, 1), ra.at[k, 3], right)
                self.send(i, 1, part(left, 1), ra.at[k, 1], left)
                self.send(i, 1, part(right, 0), ra.at[k, 0], right)
            if stage == 2:
                self.send(i, 2, part(left, 0), self.rb[i].at[k, 0], left)
                self.send(i, 2, part(right, 1), self.rb[i].at[k, 1], right)
            if stage == 6:
                for place in (left, right):
                    mine = part(xyz, 0, q1)
                    self.send(i, 6, mine, mine, place)
            if stage == 7:
                for place, src in ((right, part(left, 0)), (left, part(right, 1))):
                    self.send(i, 7, src, src, place)
            for by in (2, 1, 3):
                if stage == 3:
                    src = hx.at[pl.ds(xyz[k] * q1 + at[by][axis] * q2, q2), cols]
                    self.send(i, 3, src, self.r2[i].at[k, by - 1], at[by])
                if stage == 4:
                    src = self.r3[i].at[k, xyz[axis]]
                    self.send(i, 4, src, src, at[by])
                if stage == 5:
                    src = hx.at[pl.ds(xyz[k] * q1 + xyz[axis] * q2, q2), cols]
                    self.send(i, 5, src, src, at[by])

    def add_in(self, i, first, k, size, terms):
        step = min(size, 96)
        hx = self.hx[i]

        def body(j):
            rows = pl.ds(pl.multiple_of(first + j * step, 16), step)
            v = hx[rows, pl.ds(k * 256, 256)].astype(f32)
            for ref, at in terms:
                v = v + ref[k, at, span(j, step), :].astype(f32)
            hx[rows, pl.ds(k * 256, 256)] = v.astype(bf16)

        loop(size // step, body)

    def take(self, i, stage):
        hx, xyz = self.hx[i], self.xyz
        _, q1, half, q2 = self.sizes(i)
        if stage == 0:
            for b in range(BLOCKS[i]):
                rows = slice(b * BLOCK, (b + 1) * BLOCK)
                self.wait(i, STAGES + b, self.gs.at[b])
                self.wait(i, STAGES + b, self.gs.at[b], sent=True)

                def body(j):
                    r = span(j, 96)
                    at = span(j, 96, b * BLOCK)
                    hx[at, :] = (self.go[SLOTS[i] + b, r, :].astype(f32) + hx[at, :].astype(f32)).astype(bf16)

                loop(BLOCK // 96, body)
            return
        self.wait(i, stage, self.amount(i, stage))
        self.wait(i, stage, self.amount(i, stage), sent=True)
        for k in range(3):
            own = xyz[k] * q1
            if stage == 1:
                left, right = along(xyz, k, 3)[k], along(xyz, k, 1)[k]
                self.add_in(i, left * q1, k, half, [(self.ra[i], 2)])
                self.add_in(i, right * q1 + half, k, half, [(self.ra[i], 3)])
            if stage == 2:
                self.add_in(i, own, k, half, [(self.ra[i], 0), (self.rb[i], 0)])
                self.add_in(i, own + half, k, half, [(self.ra[i], 1), (self.rb[i], 1)])
            if stage == 3:
                first = pl.multiple_of(own + xyz[(k + 1) % 3] * q2, 16)
                v = hx[pl.ds(first, q2), pl.ds(k * 256, 256)].astype(f32)
                for d in range(3):
                    v = v + self.r2[i][k, d].astype(f32)
                self.r3[i][k, xyz[(k + 2) % 3]] = v.astype(bf16)
            if stage == 4:
                v = self.r3[i][k, 0].astype(f32)
                for d in range(1, 4):
                    v = v + self.r3[i][k, d].astype(f32)
                first = pl.multiple_of(own + xyz[(k + 1) % 3] * q2, 16)
                hx[pl.ds(first, q2), pl.ds(k * 256, 256)] = v.astype(bf16)

    def advance(self, i, stage):
        self.take(i, stage - 1)
        self.start(i, stage)

    def finish(self):
        for i in range(len(BLOCKS)):
            self.wait(i, 8, self.hx[i])
            pltpu.make_async_copy(self.hx[i], self.hx[i], self.lsem.at[i]).wait()
            self.wait(i, 8, self.hx[i], sent=True)


    def tiny_copies(self, step):
        core, xyz = self.core, self.xyz
        part = self.tbuf.at[step, core if step == 0 else xyz[step - 1]]
        pairs = [(device(xyz, 1 - core), 0)]
        if step > 0:
            pairs = [(device(along(xyz, step - 1, by), core), by - 1) for by in (2, 1, 3)]
        return [
            remote(part, part, self.tsem.at[0, step, j], self.tsem.at[1, step, j], target)
            for target, j in pairs
        ]

    def tiny_stage(self, step):
        if step == 0:
            self.tbuf[0, self.core] = self.tiny[...]
        else:
            for copy in self.tiny_copies(step - 1):
                copy.wait()
            v = self.tbuf[step - 1, 0]
            for d in range(1, 2 if step == 1 else 4):
                v = v + self.tbuf[step - 1, d]
            if step < 4:
                self.tbuf[step, self.xyz[step - 1]] = v
            else:
                self.tiny[...] = v
        if step < 4:
            for copy in self.tiny_copies(step):
                copy.start()


COMM_SCRATCH = [
    pltpu.VMEM((4, BLOCK, D), bf16),
    pltpu.VMEM((4, BLOCK, D), bf16),
    pltpu.SemaphoreType.DMA((len(BLOCKS), STAGES + 4)),
    pltpu.SemaphoreType.DMA((len(BLOCKS), STAGES + 4)),
    pltpu.SemaphoreType.DMA((len(BLOCKS),)),
    pltpu.VMEM((16, D), f32),
    pltpu.VMEM((4, 4, 16, D), f32),
    pltpu.SemaphoreType.DMA((2, 4, 3)),
    *[pltpu.VMEM((n * BLOCK, D), bf16) for n in BLOCKS],
    *[pltpu.VMEM((3, 4, n * BLOCK // 8, 256), bf16) for n in BLOCKS[:2]],
    *[pltpu.VMEM((3, 2, n * BLOCK // 8, 256), bf16) for n in BLOCKS[:2]],
    *[pltpu.VMEM((3, 3, n * BLOCK // 16, 256), bf16) for n in BLOCKS[:2]],
    *[pltpu.VMEM((3, 4, n * BLOCK // 16, 256), bf16) for n in BLOCKS[:2]],
]

SCHEDULE = {
    "dUa": [(D_, 1)],
    "dA2": [(U_, 1), (D_, 2)],
    "att0": [(U_, 2)],
    "att1a": [(D_, 3)],
    "att2a": [(U_, 3)],
    "att3a": [(D_, 4)],
    "att4a": [(U_, 4)],
    "att5a": [(D_, 5)],
    "A": [(U_, 5)],
    "B": [(A_, 1), (D_, 6)],
    "dA1": [(B_, 1), (U_, 6)],
    "N1": [(A_, 2)],
    "P": ["t0"],
    "back": [(P_, 1), (D_, 7), "t1"],
    "out0": [(B_, 2)],
    "out1": ["t2"],
    "out2": [(U_, 7)],
    "end": [(A_, 3), (D_, 8), "t3", (P_, 2), "r0", (B_, 3), "r1", "t4", (U_, 8), "r2", (A_, 4), "r3", (P_, 3),
        "r4", (B_, 4), "r5", (A_, 5), "r6", (P_, 4), (B_, 5), (A_, 6), (P_, 5), (B_, 6), (A_, 7), (P_, 6),
        (B_, 7), (A_, 8), (P_, 7), (B_, 8), (P_, 8)],
}

WO = 3 * D
WP = 4 * D


def layer_kernel(
    assignment, image_class, caption_length,
    cotangent, states, proj_w, qkv_w, out_w, up_w, down_w,
    cls, proj_b, attn_gain, attn_shift, query_b, value_b, out_b, mlp_gain, mlp_shift, up_b, down_b,
    layer_out, o0, o1, o2, o3, o4, tiny_o, back_o, xh1_o, h_o,
    W, GA, GB, GC, dy, xh, a1, a2, raw, stc, stt, da, dh, acc, dq_s, kt, lsem, bsem, *comm_scratch,
):
    comm = Comm(comm_scratch, (o0, o1, o2, o3, o4))
    xyz, core, tiny, emit = comm.xyz, comm.core, comm.tiny, comm.emit
    partner = device(along(xyz, 0, 2), core)
    side, kept, images, captions = item_sizes(assignment, image_class, caption_length, xyz, core)

    def hook(name):
        for due in SCHEDULE.get(name, ()):
            if isinstance(due, str):
                number = int(due[1])
                if due[0] == "t":
                    comm.tiny_stage(number)
                else:
                    returned(number).start()
            else:
                comm.advance(*due)

    def hook_at(step, names):
        for at in range(6):
            if SCHEDULE.get(names % at):

                @pl.when(step == at)
                def _():
                    hook(names % at)

    def columns(ref, count, first=0):
        return [ref.at[:, b * D : b * D + D] for b in range(first, first + count)]

    def weight_rows(first, count):
        return [W.at[first + b * D : first + b * D + D] for b in range(count)]

    def load_attention():
        load.start("wqkv", *zip(columns(qkv_w, 3), weight_rows(0, 3)))
        load.start("wo", (out_w, W.at[WO : WO + D]))

    def load_proj():
        load.start("pw", *zip([proj_w.at[0], proj_w.at[1]], weight_rows(WP, 2)))

    load = Loads(lsem)
    x, h, sent = a2, da, comm.gs.at[0, 0:SLOT]
    sg, dp = [[GC.at[b, 0:SLOT] for b in pair] for pair in ((0, 1), (2, 3))]
    load.start("states", *[(states.at[0, 0, b], sg[b]) for b in range(2)])
    load_proj()
    load_attention()
    load.start("wu2", *zip(columns(up_w, 2, 2), weight_rows(FF + 2 * D, 2)))
    comm.greet()
    load("states")
    sent[...] = jnp.where(kept == 0, sg[1][...], sg[0][...])
    pieces = ((0, 176), (176, 160))
    exchange = [
        remote(sent.at[a : a + n], raw.at[side, a : a + n], bsem.at[4, j], bsem.at[5, j], partner)
        for j, (a, n) in enumerate(pieces)
    ]
    for copy in exchange:
        copy.start()
    raw[side] = jnp.where(kept == 0, sg[0][...], sg[1][...])

    def valid_rows():
        row = lax.broadcasted_iota(jnp.int32, (NR, 1), 0)
        return row, valid_of(row, images, captions)

    key_row = lax.broadcasted_iota(jnp.int32, (1, NR), 1)
    key_bias_row = jnp.where(valid_of(key_row, images, captions), 0.0, MASKED)
    thirds = [slice(j * 256, j * 256 + 256) for j in range(3)]
    gain1, shift1 = row_of(attn_gain), row_of(attn_shift)
    query_bias, value_bias = row_of(query_b), row_of(value_b)
    half_lane = lax.broadcasted_iota(jnp.int32, (QUERY_ROWS, 128), 1)

    def normed(values, rows, gain, shift, a_ref, stat_lane):
        center, scale = stats(values)
        unit = center * scale
        xh[rows, :] = unit.astype(bf16)
        a_ref[rows, :] = (unit * gain + shift).astype(bf16)
        lanes = lax.broadcasted_iota(jnp.int32, (values.shape[0], 128), 1)
        stc[rows, :] = jnp.where(lanes == stat_lane, scale, stc[rows, :])

    def qkv(rows):
        a = a1[rows, :]
        for part in range(3):
            for cols in thirds:
                m = dot(a, W[part * D : part * D + D, cols])
                if part == 0:
                    m = (m + query_bias[:, cols]) * 0.125
                if part == 2:
                    m = m + value_bias[:, cols]
                GC[part, rows, cols] = m.astype(bf16)

    stc[...] = jnp.zeros_like(stc)

    def one_side(which, start, count):
        rows = pl.ds(pl.multiple_of(which * SLOT + start, 16), count)
        limit = jnp.where(which == 0, images, captions)
        keep = lax.broadcasted_iota(jnp.int32, (count, 1), 0) + start < limit
        bias = jnp.where(which == 0, proj_b[0:1, :].astype(f32), proj_b[1:2, :].astype(f32))
        inputs = raw[which, start : start + count, :]
        first = pl.multiple_of(WP + which * D, 16)
        for cols in thirds:
            p = (dot(inputs, W[pl.ds(first, D), cols]) + bias[:, cols]).astype(bf16)
            x[rows, cols] = jnp.where(keep, p, 0).astype(bf16)
        normed(x[rows, :].astype(f32), rows, gain1, shift1, a1, 12)
        qkv(rows)

    x[CLS:NR, :] = jnp.where(
        lax.broadcasted_iota(jnp.int32, (NR - CLS, 1), 0) == 0, row_of(cls), 0.0
    ).astype(bf16)
    normed(x[CLS:NR, :].astype(f32), slice(CLS, NR), gain1, shift1, a1, 12)
    load("pw")
    load("wqkv")
    qkv(slice(CLS, NR))
    one_side(side, 0, 176)
    one_side(side, 176, 160)
    row, valid_col = valid_rows()
    for cols in thirds:
        dh[0:SEQ, cols] = cotangent[0, 0, :, cols].astype(f32)
        v = dh[:, cols]
        v = jnp.where(row == CLS, v[0:1, :], pltpu.roll(v, NR - 1, 0))
        dy[:, cols] = jnp.where(valid_col, v, 0.0).astype(bf16)
    for copy, (a, n) in zip(exchange, pieces):
        copy.wait()
        one_side(1 - side, a, n)
    load.start("wu0", *zip(columns(up_w, 2), weight_rows(FF, 2)))
    load.start("xh1 out", (xh, xh1_o))

    queries, keys, values, attended = (GC.at[b] for b in range(4))

    def attend(p, block):
        rows, cols = slice(block * QUERY_ROWS, (block + 1) * QUERY_ROWS), span(p, 128)
        qq, kk, vv = queries[rows, cols], keys[:, cols], values[:, cols]
        both, kept_stats = [], stc[rows, :]
        for head in range(2):
            q_of = jnp.where(half_lane // 64 == head, qq, 0).astype(bf16)
            s = dot(q_of, kk, NT) + key_bias_row
            peak = jnp.max(s, axis=-1, keepdims=True)
            e = jnp.exp(s - peak)
            total = jnp.sum(e, axis=-1, keepdims=True)
            both.append(dot(e.astype(bf16), vv) * (1.0 / total))
            kept_stats = jnp.where(half_lane == 2 * p + head, peak + jnp.log(total), kept_stats)
        attended[rows, cols] = jnp.where(half_lane < 64, both[0], both[1]).astype(bf16)
        stc[rows, :] = kept_stats

    def attend_pairs(i):
        for p in range(1):
            for block in range(NR // QUERY_ROWS):
                attend(i * 1 + p, block)

    loop(6, attend_pairs)
    load("wo")
    out_bias = row_of(out_b)
    for cols in thirds:
        h[:, cols] = x[:, cols].astype(f32) + dot(attended[...], W[WO : WO + D, cols]) + out_bias[:, cols]
    load.start("wd", (down_w, W.at[0:FF]))
    load.start("h out", (h, h_o))
    load("xh1 out")
    gain2, shift2 = row_of(mlp_gain), row_of(mlp_shift)
    for i in range(NR // NORM_ROWS):
        rows = slice(i * NORM_ROWS, (i + 1) * NORM_ROWS)
        normed(h[rows, :], rows, gain2, shift2, a2, 13)
    load("wu2")
    load("wu0")
    up_bias = row_of(up_b)
    for b in range(4):
        for cols in thirds:
            u = dot(a2[...], W[FF + b * D : FF + b * D + D, cols])
            u = u + up_bias[:, b * D + cols.start : b * D + cols.stop]
            value, slope = gelu_both(u)
            GA[b, :, cols] = value.astype(bf16)
            GB[b, :, cols] = slope.astype(bf16)

    ones = jnp.ones((16, NR), bf16)

    def column_sums(at, value):
        tiny[at : at + 1, :] = dot(ones[:, : value.shape[0]], value)[0:1, :]

    def weight_grad(i, b, left, right):
        emit(i, b, lambda first: dot(left[:, pl.ds(first, BLOCK)], right[...], TN))

    for b in range(4):
        weight_grad(D_, b, GA.at[b], dy)
    hook("D")
    column_sums(14, dy[...])
    load("wd")
    load("h out")

    def gate_grad(b):
        for cols in thirds:
            v = dot(dy[...], W[b * D + cols.start : b * D + cols.stop, :], NT)
            GB[b, :, cols] = (v * GB[b, :, cols].astype(f32)).astype(bf16)

    gate_grad(0)
    gate_grad(1)
    hook("dUa")
    gate_grad(2)
    gate_grad(3)
    hook("dUb")
    load_attention()
    for b in range(4):
        weight_grad(U_, b, a2, GB.at[b])
        column_sums(10 + b, GB[b])
    hook("U")

    def input_grad(first, blocks):
        for cols in thirds:
            v = dot(GB[0], W[first + cols.start : first + cols.stop, :], NT)
            for b in range(1, blocks):
                v = v + dot(GB[b], W[first + b * D + cols.start : first + b * D + cols.stop, :], NT)
            da[:, cols] = v

    input_grad(FF, 4)
    load_proj()
    hook("dA2")

    def norm_back(gain_ref, xh_ref, stat_lane, add_to, at):
        gain = row_of(gain_ref)
        acc[...] = jnp.zeros_like(acc)
        for i in range(NR // NORM_ROWS):
            rows = slice(i * NORM_ROWS, (i + 1) * NORM_ROWS)
            d, xh, scale = da[rows, :], xh_ref[rows, :].astype(f32), stc[rows, stat_lane : stat_lane + 1]
            gg = d * gain
            m1 = jnp.mean(gg, axis=-1, keepdims=True)
            m2 = jnp.mean(gg * xh, axis=-1, keepdims=True)
            dh[rows, :] = add_to(rows) + scale * (gg - m1 - xh * m2)
            acc[0] += jnp.sum((d * xh).reshape(NORM_ROWS // 8, 8, D), axis=0)
            acc[1] += jnp.sum(d.reshape(NORM_ROWS // 8, 8, D), axis=0)
        tiny[at : at + 1, :] = jnp.sum(acc[0], axis=0, keepdims=True)
        tiny[at + 1 : at + 2, :] = jnp.sum(acc[1], axis=0, keepdims=True)

    norm_back(mlp_gain, xh, 13, lambda rows: dy[rows, :].astype(f32), 8)
    dy[...] = dh[...].astype(bf16)
    load.start("xh1", (xh1_o, xh))
    hook("N2")
    d_q, d_k, d_v, d_o = (GB.at[b] for b in range(4))
    load("wo")
    for cols in thirds:
        d_o[:, cols] = dot(dy[...], W[WO + cols.start : WO + cols.stop, :], NT).astype(bf16)
    weight_grad(A_, 0, attended, dy)
    column_sums(7, dy[...])
    hook("dO")
    stt[...] = jnp.transpose(stc[...])
    key_bias = jnp.where(valid_rows()[1], 0.0, MASKED)
    lane = lax.broadcasted_iota(jnp.int32, (NR, 128), 1)
    head_of = lax.broadcasted_iota(jnp.int32, (16, 128), 1) // 64
    select = (head_of == lax.broadcasted_iota(jnp.int32, (16, 128), 0)).astype(bf16)

    def attend_back(p):
        cols = span(p, 128)
        qq, do = queries[:, cols], d_o[:, cols]
        product = do.astype(f32) * attended[:, cols].astype(f32)
        high = product.astype(bf16)
        low = (product - high.astype(f32)).astype(bf16)
        delta = dot(select, high, NT) + dot(select, low, NT)
        for kb in range(NR // KEY_ROWS):
            kt[kb] = jnp.transpose(keys[kb * KEY_ROWS : (kb + 1) * KEY_ROWS, cols])
        q_of = [jnp.where(lane // 64 == head, qq, 0).astype(bf16) for head in range(2)]
        do_of = [jnp.where(lane // 64 == head, do, 0).astype(bf16) for head in range(2)]
        dq = [0.0, 0.0]
        for kb in range(NR // KEY_ROWS):
            rows = slice(kb * KEY_ROWS, (kb + 1) * KEY_ROWS)
            kk, vv = keys[rows, cols], values[rows, cols]
            dk = dv = 0.0
            for head in range(2):
                s = dot(kk, q_of[head], NT) + key_bias[rows] - stt[pl.ds(2 * p + head, 1), :]
                pr = jnp.exp(s)
                dpr = dot(vv, do_of[head], NT)
                ds = (pr * (dpr - delta[head : head + 1, :])).astype(bf16)
                dv = dv + dot(pr.astype(bf16), do_of[head])
                dk = dk + dot(ds, q_of[head])
                dq[head] = dq[head] + dot(kt[kb, head * 64 : head * 64 + 64, :], ds)
            d_k[rows, cols] = dk.astype(bf16)
            d_v[rows, cols] = dv.astype(bf16)
            if kb == 0:
                hook_at(p, "att%da")
        for head in range(2):
            dq_s[head * 64 : head * 64 + 64, :] = dq[head]
        d_q[:, cols] = (jnp.transpose(dq_s[...]).astype(bf16).astype(f32) * 0.125).astype(bf16)
        hook_at(p, "att%d")

    loop(6, attend_back)
    weight_grad(A_, 1, a1, d_q)
    hook("A")
    weight_grad(B_, 0, a1, d_k)
    weight_grad(B_, 1, a1, d_v)
    hook("B")
    column_sums(5, d_q[...])
    column_sums(6, d_v[...])
    load("wqkv")
    input_grad(0, 3)
    load.start("wd2", (down_w, W.at[0:FF]))
    hook("dA1")
    load("xh1")
    norm_back(attn_gain, xh, 12, lambda rows: dh[rows, :], 3)
    load.start("h", (h_o, da))
    tiny[0:1, :] = dh[CLS : CLS + 1, :]
    tiny[15:16, :] = jnp.zeros((1, D), f32)
    hook("N1")
    for s in range(2):
        dp[s][...] = dh[s * SLOT : (s + 1) * SLOT, :].astype(bf16)
    for s in range(2):
        weight_grad(P_, s, raw.at[s], dp[s])
        column_sums(1 + s, dp[s][...])
    hook("P")
    load("pw")

    def states_back(which, slot):
        for j in range(3):
            v = dot(GC[2 + which, 0:SLOT, :], W[span(j, 256, WP + which * D), :], NT)
            sg[slot][:, j * 256 : j * 256 + 256] = v.astype(bf16)

    def returned(piece):
        rows = pl.ds(piece * 48, 48)
        return remote(
            sg[1].at[rows], back_o.at[1, rows], bsem.at[0, piece], bsem.at[1, piece], partner
        )

    states_back(1 - side, 1)
    states_back(side, 0)
    own = pltpu.make_async_copy(sg[0], back_o.at[0], bsem.at[2, 0])
    own.start()
    hook("back")
    load("wd2")
    load("h")
    down_bias = row_of(down_b)
    row, valid_col = valid_rows()
    valid = valid_col.astype(f32)
    for cols in thirds:
        y = da[:, cols] + down_bias[:, cols]
        for b in range(4):
            y = y + dot(GA[b], W[b * D : b * D + D, cols])
        y = y * valid
        y = jnp.where(row == 0, y[CLS : CLS + 1, :], pltpu.roll(y, 1, 0))
        layer_out[0, 0, :, cols] = y[:SEQ].astype(bf16)
        hook("out%d" % (cols.start // 256))
    hook("end")
    final = pltpu.make_async_copy(tiny, tiny_o, bsem.at[3, 0])
    final.start()
    comm.finish()
    final.wait()
    own.wait()
    for piece in range(7):
        returned(piece).wait()


PIECE = 768


def unpack_kernel(
    assignment, back, c0, c1, c2, c3, c4, tiny_i,
    states_grad, cls, proj_w, proj_b, attn_gain, attn_shift, qkv_w, query_b, value_b, out_w, out_b,
    mlp_gain, mlp_shift, up_w, up_b, down_w, down_b,
    src, dst, tiny, pair, isem, osem, bsem,
):
    xyz, core = coords()
    side = xyz[0] // 2
    group = ((lax.rem(xyz[0], 2) * 2 + xyz[2] // 2) * 4 + xyz[1]) * 2 + core
    chosen = assignment[0, group]
    kept = jnp.where(side == 0, chosen, 1 - chosen)
    moves = [
        pltpu.make_async_copy(back, pair, bsem.at[0]),
        pltpu.make_async_copy(pair.at[0], states_grad.at[0, 0, kept], bsem.at[1]),
        pltpu.make_async_copy(pair.at[1], states_grad.at[0, 0, 1 - kept], bsem.at[2]),
        pltpu.make_async_copy(tiny_i, tiny, bsem.at[3]),
    ]
    moves[0].start()
    moves[3].start()
    blocks = []
    for b in range(4):
        blocks.append((c0, b, down_w.at[b * D : b * D + D]))
    for b in range(4):
        blocks.append((c1, b, up_w.at[:, b * D : b * D + D]))
    blocks.append((c2, 0, out_w))
    for b, (chunk, at) in enumerate(((c2, 1), (c3, 0), (c3, 1))):
        blocks.append((chunk, at, qkv_w.at[:, b * D : b * D + D]))
    for b in range(2):
        blocks.append((c4, b, proj_w.at[b]))
    n = len(blocks)
    depth = 4

    def read(i):
        chunk, at, _ = blocks[i]
        return pltpu.make_async_copy(chunk.at[at * D : at * D + D], src.at[i % depth], isem.at[i % depth])

    def write(i):
        return pltpu.make_async_copy(dst.at[i % depth], blocks[i][2], osem.at[i % depth])

    for i in range(depth):
        read(i).start()
    for i in range(n):
        if i == 2:
            moves[0].wait()
            moves[1].start()
            moves[2].start()
        read(i).wait()
        if i >= depth:
            write(i - depth).wait()

        def body(j):
            dst[i % depth, span(j, 64), :] = src[i % depth, span(j, 64), :].astype(f32)

        loop(D // 64, body)
        write(i).start()
        if i + depth < n:
            read(i + depth).start()
    moves[3].wait()
    for ref, at in ((cls, 0), (attn_gain, 3), (attn_shift, 4), (query_b, 5), (value_b, 6), (out_b, 7), (mlp_gain, 8), (mlp_shift, 9), (down_b, 14)):
        ref[...] = tiny[at : at + 1, :].reshape(D)
    proj_b[...] = tiny[1:3, :]
    for b in range(4):
        up_b[pl.ds(b * D, D)] = tiny[10 + b : 11 + b, :].reshape(D)
    for i in range(n - depth, n):
        write(i).wait()
    moves[1].wait()
    moves[2].wait()


def shape(*dims, dtype=bf16):
    return jax.ShapeDtypeStruct(dims, dtype)


def scratch(*dims, dtype=bf16):
    return pltpu.VMEM(dims, dtype)


ANY = pl.BlockSpec(memory_space=pl.ANY)
VMEM = pl.BlockSpec(memory_space=pltpu.VMEM)
SMEM = pl.BlockSpec(memory_space=pltpu.SMEM)
DMA = pltpu.SemaphoreType.DMA
ITEM = (NR, D)


def per_device(
    side_states, assignment, image_class, caption_length, cls_token, proj_weight, proj_bias,
    attn_gain, attn_shift, qkv_weight, query_bias, value_bias, out_weight, out_bias,
    mlp_gain, mlp_shift, up_weight, up_bias, down_weight, down_bias, out_cotangent,
):
    sizes = (assignment, jnp.swapaxes(image_class, 1, 2), jnp.swapaxes(caption_length, 1, 2))
    layer_out, *chunks, tiny, back, _, _ = pl.pallas_call(
        layer_kernel,
        out_shape=[shape(1, 1, SEQ, D)]
        + [shape(n * D, D) for n in BLOCKS]
        + [shape(16, D, dtype=f32), shape(2, SLOT, D), shape(*ITEM), shape(*ITEM, dtype=f32)],
        in_specs=[SMEM] * 3 + [VMEM] + [ANY] * 6 + [VMEM] * 11,
        out_specs=[VMEM] + [ANY] * (len(BLOCKS) + 4),
        scratch_shapes=[
            scratch(8 * D, D), scratch(4, *ITEM), scratch(4, *ITEM), scratch(4, *ITEM),
            scratch(*ITEM), scratch(*ITEM), scratch(*ITEM), scratch(*ITEM), scratch(2, SLOT, D),
            scratch(NR, 128, dtype=f32), scratch(128, NR, dtype=f32),
            scratch(*ITEM, dtype=f32), scratch(*ITEM, dtype=f32),
            scratch(2, 8, D, dtype=f32), scratch(128, NR, dtype=f32), scratch(2, 128, KEY_ROWS),
            DMA((40,)), DMA((6, 7)), *COMM_SCRATCH,
        ],
        compiler_params=pltpu.CompilerParams(
            collective_id=0, has_side_effects=True, vmem_limit_bytes=63 * MIB
        ),
        name="layer",
    )(
        *sizes, out_cotangent, side_states, proj_weight, qkv_weight, out_weight, up_weight, down_weight,
        cls_token, proj_bias, attn_gain, attn_shift, query_bias, value_bias, out_bias,
        mlp_gain, mlp_shift, up_bias, down_bias,
    )
    vector = shape(D, dtype=f32)
    grads = pl.pallas_call(
        unpack_kernel,
        out_shape=[
            shape(1, 1, 2, SLOT, D), vector, shape(2, D, D, dtype=f32), shape(2, D, dtype=f32), vector, vector,
            shape(D, 3 * D, dtype=f32), vector, vector, shape(D, D, dtype=f32), vector, vector, vector,
            shape(D, FF, dtype=f32), shape(FF, dtype=f32), shape(FF, D, dtype=f32), vector,
        ],
        in_specs=[SMEM] + [ANY] * (len(BLOCKS) + 2),
        out_specs=[ANY, VMEM, ANY, VMEM, VMEM, VMEM, ANY, VMEM, VMEM, ANY, VMEM, VMEM, VMEM, ANY, VMEM, ANY, VMEM],
        scratch_shapes=[
            scratch(4, PIECE, D), scratch(4, PIECE, D, dtype=f32), scratch(16, D, dtype=f32), scratch(2, SLOT, D),
            DMA((4,)), DMA((4,)), DMA((4,)),
        ],
        compiler_params=pltpu.CompilerParams(vmem_limit_bytes=62 * MIB),
        name="unpack",
    )(assignment, back, *chunks, tiny)
    return (layer_out, *grads)


def solution(mesh):
    weights = (P(),) * 16
    return jax.shard_map(
        per_device,
        mesh=mesh,
        in_specs=(P("items", "tower"), P("items"), P("items"), P("items"), *weights, P("items", "tower")),
        out_specs=(P("items", "tower"), P("items", "tower"), *weights),
        check_vma=False,
    )
```
